256 devices in a mesh: strike: 32 (over x_lo, z, core), depth: 8 (over x_hi, y).
Axes of the slice: x: 4 (x_hi: 2, x_lo: 2; x = x_hi * 2 + x_lo), y: 4, z: 8, core: 2. Of those that a mesh axis runs over, the one named last changes fastest.
Arguments:
- sliding_speed: float32 [768, 8192], P('depth', 'strike'), may hold values from 0.1 to 10
- offset_displacement: float32 [768, 8192], P('depth', 'strike'), may hold values from -6 to 6
- contact_memory: float32 [768, 8192], P('depth', 'strike'), may hold values from -1 to 1
- clamping_traction: float32 [768, 8192], P('depth', 'strike'), may hold values from 5 to 9
- instant_effect_a: float32 [768, 8192], P('depth', 'strike'), may hold values from 0.5 to 1
- healing_effect_b: float32 [768, 8192], P('depth', 'strike'), may hold values from 0.5 to 1.5
- ambient_traction: float32 [768, 8192], P('depth', 'strike'), may hold values from 0 to 10
- heat_level: float32 [32, 768, 8192], P(None, 'depth', 'strike'), may hold values from -4 to 4
- fluid_load: float32 [32, 768, 8192], P(None, 'depth', 'strike'), may hold values from -4 to 4
Outputs:
- sliding_acceleration: float32 [768, 8192], P('depth', 'strike')
- memory_change: float32 [768, 8192], P('depth', 'strike')
- heat_level_change: float32 [32, 768, 8192], P(None, 'depth', 'strike')
- fluid_load_change: float32 [32, 768, 8192], P(None, 'depth', 'strike')
The draws below stay inside these ranges and needn't reach their ends.
All inputs are finite; a program needn't handle non-finite values.
Results may differ from the reference program's by a relative error of at most 0.00005.
Values sent between devices are 32-bit elements; how exact they have to be, the bound alone decides.
No kernel may reach another device: no remote copies, remote signals or barrier semaphores. Data moves between devices by JAX's collectives and lax.ppermute only.
A program may use at most 128 MiB of HBM per device.

```python
import math
import jax
import jax.numpy as jnp

ALONG_COUNT = 8192
DOWNDIP_COUNT = 768
ACROSS_SAMPLES = 32


def steps_of(rng, dims, shards, low, high):
    loudness, own = 1.0, jax.random.fold_in(rng, 6)
    for axis_at, shards_of in shards:
        steps = jnp.exp(jax.random.uniform(jax.random.fold_in(own, axis_at), (shards_of,), jnp.float32, low / len(shards), high / len(shards)))
        loudness = loudness * jnp.repeat(steps, dims[axis_at] // shards_of).reshape([-1 if axis == axis_at else 1 for axis in range(len(dims))])
    return loudness


def bell_draw(own_key, dims, scale, bound, split=(), kind=jnp.bfloat16):
    drawn = jax.random.normal(own_key, dims, jnp.float32) * scale
    if len(split) > 0:
        drawn = steps_of(own_key, dims, split, -0.22, 0.18) * drawn
    return jnp.clip(drawn, min=-bound, max=bound).astype(kind)


def setup_inputs(seed: int = 0) -> dict:
    streams_of = jax.random.split(jax.random.key(seed), 10)
    return {
        "sliding_speed": jnp.clip(jnp.exp(math.log(10.0) - 4.6051702 * jax.random.uniform(streams_of[0], (DOWNDIP_COUNT, ALONG_COUNT), jnp.float32) ** steps_of(streams_of[0], (DOWNDIP_COUNT, ALONG_COUNT), ((0, 8), (1, 32)), -0.2, 0.2)), 0.1, 10.0),
        "offset_displacement": bell_draw(streams_of[1], (DOWNDIP_COUNT, ALONG_COUNT), 1.0, 6.0, ((0, 8), (1, 32)), jnp.float32),
        "contact_memory": jnp.clip(jax.random.uniform(streams_of[2], (DOWNDIP_COUNT, ALONG_COUNT), jnp.float32, -1.0, 1.0) * steps_of(streams_of[2], (DOWNDIP_COUNT, ALONG_COUNT), ((0, 8), (1, 32)), -0.4, 0.0), -1.0, 1.0),
        "clamping_traction": jnp.clip(jnp.exp(math.log(9.0) - 0.5877867 * jax.random.uniform(streams_of[3], (DOWNDIP_COUNT, ALONG_COUNT), jnp.float32) ** steps_of(streams_of[3], (DOWNDIP_COUNT, ALONG_COUNT), ((0, 8), (1, 32)), -0.2, 0.2)), 5.0, 9.0),
        "instant_effect_a": jnp.clip(jnp.exp(math.log(1.0) - 0.6931472 * jax.random.uniform(streams_of[4], (DOWNDIP_COUNT, ALONG_COUNT), jnp.float32) ** steps_of(streams_of[4], (DOWNDIP_COUNT, ALONG_COUNT), ((0, 8), (1, 32)), -0.2, 0.2)), 0.5, 1.0),
        "healing_effect_b": jnp.clip(jnp.exp(math.log(1.5) - 1.0986123 * jax.random.uniform(streams_of[5], (DOWNDIP_COUNT, ALONG_COUNT), jnp.float32) ** steps_of(streams_of[5], (DOWNDIP_COUNT, ALONG_COUNT), ((0, 8), (1, 32)), -0.2, 0.2)), 0.5, 1.5),
        "ambient_traction": jnp.clip(10.0 * jax.random.uniform(streams_of[6], (DOWNDIP_COUNT, ALONG_COUNT), jnp.float32) ** steps_of(streams_of[6], (DOWNDIP_COUNT, ALONG_COUNT), ((0, 8), (1, 32)), -0.2, 0.2), 0.0, 10.0),
        "heat_level": bell_draw(streams_of[7], (ACROSS_SAMPLES, DOWNDIP_COUNT, ALONG_COUNT), 0.5, 4.0, ((1, 8), (2, 32)), jnp.float32),
        "fluid_load": bell_draw(streams_of[8], (ACROSS_SAMPLES, DOWNDIP_COUNT, ALONG_COUNT), 0.5, 4.0, ((1, 8), (2, 32)), jnp.float32),
    }


HEAT_GAIN = 0.05
HEAT_DIFFUSIVITY = 0.3
FLUID_DIFFUSIVITY = 0.45
FLUID_TOGGLE = 0.6
REF_FRICTION = 0.5
DAMPING = 0.5
RELAXATION = 0.2
ELASTIC = 4.0 / 3.0
HEAT_WIDTH = 4.0

def discrete_laplacian(values_in):
    above_part = jnp.concatenate([values_in[1:], jnp.zeros_like(values_in[:1])], 0)
    below_part = jnp.concatenate([values_in[1:2], values_in[:-1]], 0)
    return above_part - 2.0 * values_in + below_part

def interface_tendencies(sliding_speed, contact_memory, clamping_traction, instant_effect_a, healing_effect_b, heat_level, fluid_load):
    argument = 0.5 * sliding_speed * jnp.exp(contact_memory / instant_effect_a)
    friction = instant_effect_a * jnp.log(argument + jnp.sqrt(argument * argument + 1.0))
    root_term = jnp.sqrt(4.0 * jnp.exp(-2.0 * contact_memory / instant_effect_a) + sliding_speed * sliding_speed)
    effective = clamping_traction - fluid_load[0]
    sliding_traction = effective * friction
    across_sample_count = jnp.arange(heat_level.shape[0]).astype(jnp.float32)
    across_layout = jnp.exp(-(across_sample_count / HEAT_WIDTH) ** 2)
    dissipated_power = HEAT_GAIN * sliding_traction * sliding_speed
    heat_level_change = HEAT_DIFFUSIVITY * discrete_laplacian(heat_level) + across_layout[:, None, None] * dissipated_power[None]
    fluid_load_change = FLUID_DIFFUSIVITY * discrete_laplacian(fluid_load) + FLUID_TOGGLE * heat_level_change
    memory_change = healing_effect_b * (jnp.exp((REF_FRICTION - contact_memory) / healing_effect_b) - sliding_speed)
    extra_contribution = friction * fluid_load_change[0] - effective * (sliding_speed / root_term) * memory_change
    denominator_value = effective * instant_effect_a / root_term + DAMPING
    return (extra_contribution, denominator_value, sliding_traction, memory_change, heat_level_change, fluid_load_change)

def kernel_table(rows_index, cols_index, depth_total, strike_total):
    depth_mode = jnp.minimum(rows_index, depth_total - rows_index).astype(jnp.float32)
    strike_mode = jnp.minimum(cols_index, strike_total - cols_index).astype(jnp.float32)
    depth_wave = 2.0 * math.pi / depth_total * depth_mode
    strike_wave = 2.0 * math.pi / strike_total * strike_mode
    wave_square = strike_wave * strike_wave + depth_wave * depth_wave
    return -0.5 * (strike_wave * strike_wave * ELASTIC + depth_wave * depth_wave) / jnp.sqrt(jnp.where(wave_square > 0, wave_square, 1.0))

def reference(sliding_speed, offset_displacement, contact_memory, clamping_traction, instant_effect_a, healing_effect_b, ambient_traction, heat_level, fluid_load):
    extra_contribution, denominator_value, sliding_traction, memory_change, heat_level_change, fluid_load_change = interface_tendencies(sliding_speed, contact_memory, clamping_traction, instant_effect_a, healing_effect_b, heat_level, fluid_load)
    kernel = kernel_table(jnp.arange(DOWNDIP_COUNT, dtype=jnp.int32)[:, None], jnp.arange(ALONG_COUNT, dtype=jnp.int32)[None, :], DOWNDIP_COUNT, ALONG_COUNT)
    spectra = jnp.fft.fft2(jnp.stack([sliding_speed, offset_displacement]))
    filtered = jnp.real(jnp.fft.ifft2(kernel[None] * spectra)).astype(jnp.float32)
    stress_rate = filtered[0]
    elastic_stress = filtered[1]
    mismatch = ambient_traction + elastic_stress - DAMPING * sliding_speed - sliding_traction
    sliding_acceleration = (stress_rate + extra_contribution + RELAXATION * mismatch) / denominator_value
    return (sliding_acceleration, memory_change, heat_level_change, fluid_load_change)
```

```python
import math

import jax
import jax.numpy as jnp
import ml_dtypes
import numpy as np
from jax import lax
from jax.experimental import pallas as pl
from jax.experimental.pallas import tpu as pltpu
from jax.sharding import PartitionSpec as P

HEAT_GAIN = 0.05
HEAT_DIFFUSIVITY = 0.3
FLUID_DIFFUSIVITY = 0.45
FLUID_TOGGLE = 0.6
REF_FRICTION = 0.5
DAMPING = 0.5
RELAXATION = 0.2
ELASTIC = 4.0 / 3.0
HEAT_WIDTH = 4.0

DEPTH = 768
STRIKE = 8192
ROWS = 96
COLS = 256
POINTS = 32
DEPTH_PARTS = 8
STRIKE_PARTS = 32
LANES = 128
COARSE = STRIKE // LANES
CLASSES = COARSE // 2 + 1
MODES = 3
SLOTS = 4
SPEC_ROWS = 112

F32 = jnp.float32
BF16 = jnp.bfloat16


def halves(table):
    high = table.astype(ml_dtypes.bfloat16)
    low = (table - high.astype(np.float64)).astype(ml_dtypes.bfloat16)
    return high, low


def depth_table():
    index = np.arange(DEPTH)
    angle = 2.0 * np.pi / DEPTH * (index[:, None] * index[None, :] % DEPTH)
    return np.cos(angle) + np.sin(angle)


def coarse_tables():
    angle = 2.0 * np.pi / COARSE * (np.arange(CLASSES)[:, None] * np.arange(COARSE)[None, :] % COARSE)
    forward = np.zeros((2, SPEC_ROWS, COARSE, SLOTS))
    inverse = np.zeros((COARSE, SLOTS, 2, SPEC_ROWS))
    weight = np.where(np.arange(CLASSES) % (COARSE // 2) == 0, 1.0, 2.0)[:, None]
    for mode in range(MODES):
        at = np.arange(CLASSES) * MODES + mode
        forward[0, at, :, mode] = np.cos(angle)
        forward[1, at, :, mode] = -np.sin(angle)
        inverse[:, mode, 0, at] = (weight * np.cos(angle)).T
        inverse[:, mode, 1, at] = (-weight * np.sin(angle)).T
    return (
        forward.reshape(2 * SPEC_ROWS, COARSE * SLOTS),
        inverse.reshape(COARSE * SLOTS, 2 * SPEC_ROWS),
    )


def fine_tables():
    index = np.arange(LANES)
    angle = 2.0 * np.pi / LANES * (index[:, None] * index[None, :] % LANES)
    cosine, sine = np.cos(angle), np.sin(angle)
    forward = np.block([[cosine, -sine], [sine, cosine]])
    inverse = np.block([[cosine, sine], [-sine, cosine]])
    return forward, inverse


def class_tables():
    row = np.arange(SPEC_ROWS)
    k_one = np.minimum(row // MODES, CLASSES - 1)
    lane = np.arange(LANES)
    angle = 2.0 * np.pi / STRIKE * (k_one[:, None] * lane[None, :])
    wave = k_one[:, None] + COARSE * lane[None, :]
    strike_wave = 2.0 * np.pi / STRIKE * np.minimum(wave, STRIKE - wave)
    offset = np.broadcast_to((row % MODES * STRIKE_PARTS)[:, None], (SPEC_ROWS, LANES))
    return tuple(
        np.asarray(table, np.float32)
        for table in (np.cos(angle), np.sin(angle), strike_wave * strike_wave, offset)
    )


def split(values):
    high = values.astype(BF16)
    return high, (values - high.astype(F32)).astype(BF16)


def mm(left, right):
    return jnp.dot(left, right, preferred_element_type=F32)


def table_first(high, low, values):
    v_high, v_low = split(values)
    return mm(high, v_high) + (mm(high, v_low) + mm(low, v_high))


def table_last(values, high, low):
    v_high, v_low = split(values)
    return mm(v_high, high) + (mm(v_low, high) + mm(v_high, low))


def depth_kernel(fields_ref, high_ref, low_ref, out_ref):
    modes = table_first(high_ref[...], low_ref[...], fields_ref[...])
    blank = jnp.zeros((STRIKE_PARTS, LANES), F32)
    for half in range(2):
        for slot in range(SLOTS):
            piece = blank
            if slot < MODES:
                piece = modes[
                    slot * STRIKE_PARTS : (slot + 1) * STRIKE_PARTS,
                    half * LANES : (half + 1) * LANES,
                ]
            out_ref[pl.ds(half * SLOTS + slot, STRIKE_PARTS, stride=2 * SLOTS), :] = piece


def strike_kernel(
    base_ref,
    modes_ref,
    coarse_high,
    coarse_low,
    fine_high,
    fine_low,
    back_high,
    back_low,
    out_high,
    out_low,
    cos_ref,
    sin_ref,
    strike_square_ref,
    offset_ref,
    out_ref,
):
    cosine, sine = cos_ref[...], sin_ref[...]
    depth_index = offset_ref[...] + base_ref[0].astype(F32)
    depth_wave = 2.0 * math.pi / DEPTH * jnp.minimum(depth_index, DEPTH - depth_index)
    depth_square = depth_wave * depth_wave
    strike_square = strike_square_ref[...]
    wave_square = strike_square + depth_square
    kernel = (
        (-0.5 / (DEPTH * STRIKE))
        * (strike_square * ELASTIC + depth_square)
        / jnp.sqrt(jnp.where(wave_square > 0, wave_square, 1.0))
    )
    coarse = table_first(coarse_high[...], coarse_low[...], modes_ref[...])
    real, imag = coarse[:SPEC_ROWS], coarse[SPEC_ROWS:]
    turned = jnp.concatenate([real * cosine + imag * sine, imag * cosine - real * sine], 1)
    spectrum = table_last(turned, fine_high[...], fine_low[...])
    spectrum = spectrum * jnp.concatenate([kernel, kernel], 1)
    back = table_last(spectrum, back_high[...], back_low[...])
    real, imag = back[:, :LANES], back[:, LANES:]
    turned = jnp.concatenate([real * cosine - imag * sine, imag * cosine + real * sine], 0)
    out_ref[...] = table_first(out_high[...], out_low[...], turned)


def spread_kernel(modes_ref, out_ref):
    for half in range(2):
        for slot in range(MODES):
            piece = modes_ref[pl.ds(half * SLOTS + slot, STRIKE_PARTS, stride=2 * SLOTS), :]
            for part in range(DEPTH_PARTS):
                out_ref[
                    part,
                    slot * STRIKE_PARTS : (slot + 1) * STRIKE_PARTS,
                    half * LANES : (half + 1) * LANES,
                ] = piece


def final_kernel(modes_ref, high_ref, low_ref, numerator_ref, denominator_ref, out_ref):
    filtered = table_first(high_ref[...], low_ref[...], modes_ref[...])
    out_ref[...] = (filtered + numerator_ref[...]) / denominator_ref[...]


def heat_kernel(
    speed_ref,
    memory_ref,
    clamping_ref,
    effect_a_ref,
    effect_b_ref,
    ambient_ref,
    heat_ref,
    fluid_ref,
    heat_out,
    memory_out,
    numerator_out,
    denominator_out,
):
    speed, memory = speed_ref[...], memory_ref[...]
    effect_a, effect_b = effect_a_ref[...], effect_b_ref[...]
    ratio = memory / effect_a
    argument = 0.5 * speed * jnp.exp(ratio)
    friction = effect_a * jnp.log(argument + jnp.sqrt(argument * argument + 1.0))
    root_term = jnp.sqrt(4.0 * jnp.exp(-2.0 * ratio) + speed * speed)
    effective = clamping_ref[...] - fluid_ref[0]
    traction = effective * friction
    power = HEAT_GAIN * traction * speed
    memory_change = effect_b * (jnp.exp((REF_FRICTION - memory) / effect_b) - speed)
    memory_out[...] = memory_change
    for point in range(POINTS):
        here = heat_ref[point]
        above = heat_ref[point + 1] if point + 1 < POINTS else None
        below = heat_ref[point - 1] if point > 0 else heat_ref[1]
        bent = below - 2.0 * here
        if above is not None:
            bent = bent + above
        change = HEAT_DIFFUSIVITY * bent + math.exp(-((point / HEAT_WIDTH) ** 2)) * power
        heat_out[point] = change
        if point == 0:
            fluid_change = (
                FLUID_DIFFUSIVITY * (2.0 * fluid_ref[1] - 2.0 * fluid_ref[0])
                + FLUID_TOGGLE * change
            )
    extra = friction * fluid_change - effective * (speed / root_term) * memory_change
    numerator_out[...] = extra + RELAXATION * (ambient_ref[...] - DAMPING * speed - traction)
    denominator_out[...] = effective * effect_a / root_term + DAMPING


def fluid_kernel(fluid_ref, heat_change_ref, out_ref):
    for point in range(POINTS):
        here = fluid_ref[point]
        below = fluid_ref[point - 1] if point > 0 else fluid_ref[1]
        bent = below - 2.0 * here
        if point + 1 < POINTS:
            bent = bent + fluid_ref[point + 1]
        out_ref[point] = FLUID_DIFFUSIVITY * bent + FLUID_TOGGLE * heat_change_ref[point]


def whole(count):
    return [pl.BlockSpec(memory_space=pltpu.VMEM)] * count


def cost(flops, moved):
    return pl.CostEstimate(flops=flops, bytes_accessed=moved, transcendentals=0)


def shape(*dims):
    return jax.ShapeDtypeStruct(dims, F32)


BLOCK = 16


def rows_spec():
    return pl.BlockSpec((BLOCK, COLS), lambda i: (i, 0))


def points_spec(points=POINTS):
    return pl.BlockSpec((points, BLOCK, COLS), lambda i: (0, i, 0))


def shards(
    sliding_speed,
    offset_displacement,
    contact_memory,
    clamping_traction,
    instant_effect_a,
    healing_effect_b,
    ambient_traction,
    heat_level,
    fluid_load,
):
    depth_pos = lax.axis_index("depth")
    strike_pos = lax.axis_index("strike")
    depth_high, depth_low = (
        lax.dynamic_slice_in_dim(jnp.asarray(table), depth_pos * ROWS, ROWS, 0)
        for table in halves(depth_table())
    )
    coarse_forward, coarse_inverse = coarse_tables()
    fine_forward, fine_inverse = fine_tables()
    base = (depth_pos * ROWS + strike_pos).astype(jnp.int32).reshape(1)
    small = ROWS * COLS * 4

    field = sliding_speed + RELAXATION * offset_displacement
    sent = jnp.broadcast_to(field[None], (DEPTH_PARTS, ROWS, COLS))
    columns = lax.all_to_all(sent, "depth", split_axis=0, concat_axis=0)

    modes = pl.pallas_call(
        depth_kernel,
        out_shape=shape(STRIKE_PARTS * 2 * SLOTS, LANES),
        in_specs=whole(3),
        out_specs=pl.BlockSpec(memory_space=pltpu.VMEM),
        cost_estimate=cost(6 * ROWS * DEPTH * COLS, 12 * small),
    )(columns.reshape(DEPTH, COLS), depth_high, depth_low)

    modes = lax.all_to_all(
        modes.reshape(STRIKE_PARTS, 2 * SLOTS, LANES), "strike", split_axis=0, concat_axis=0
    )

    filtered = pl.pallas_call(
        strike_kernel,
        out_shape=shape(STRIKE_PARTS * 2 * SLOTS, LANES),
        in_specs=[pl.BlockSpec(memory_space=pltpu.SMEM)] + whole(13),
        out_specs=pl.BlockSpec(memory_space=pltpu.VMEM),
        cost_estimate=cost(6 * 4 * 256 * 256 * LANES, 15 * small),
    )(
        base,
        modes.reshape(STRIKE_PARTS * 2 * SLOTS, LANES),
        *halves(coarse_forward),
        *halves(fine_forward),
        *halves(fine_inverse),
        *halves(coarse_inverse),
        *class_tables(),
    )

    filtered = lax.all_to_all(
        filtered.reshape(STRIKE_PARTS, 2 * SLOTS, LANES), "strike", split_axis=0, concat_axis=0
    )

    sent = pl.pallas_call(
        spread_kernel,
        out_shape=shape(DEPTH_PARTS, ROWS, COLS),
        in_specs=whole(1),
        out_specs=pl.BlockSpec(memory_space=pltpu.VMEM),
        cost_estimate=cost(0, 9 * small),
    )(filtered.reshape(STRIKE_PARTS * 2 * SLOTS, LANES))
    columns = lax.all_to_all(sent, "depth", split_axis=0, concat_axis=0)

    heat_level_change, memory_change, numerator, denominator = pl.pallas_call(
        heat_kernel,
        grid=(ROWS // BLOCK,),
        out_shape=(
            shape(POINTS, ROWS, COLS),
            shape(ROWS, COLS),
            shape(ROWS, COLS),
            shape(ROWS, COLS),
        ),
        in_specs=[rows_spec()] * 6 + [points_spec(), points_spec(2)],
        out_specs=(points_spec(), rows_spec(), rows_spec(), rows_spec()),
        cost_estimate=cost(8 * POINTS * ROWS * COLS, 75 * small),
    )(
        sliding_speed,
        contact_memory,
        clamping_traction,
        instant_effect_a,
        healing_effect_b,
        ambient_traction,
        heat_level,
        fluid_load,
    )
    fluid_load_change = pl.pallas_call(
        fluid_kernel,
        grid=(ROWS // BLOCK,),
        out_shape=shape(POINTS, ROWS, COLS),
        in_specs=[points_spec()] * 2,
        out_specs=points_spec(),
        cost_estimate=cost(8 * POINTS * ROWS * COLS, 96 * small),
    )(fluid_load, heat_level_change)

    sliding_acceleration = pl.pallas_call(
        final_kernel,
        out_shape=shape(ROWS, COLS),
        in_specs=whole(5),
        out_specs=pl.BlockSpec(memory_space=pltpu.VMEM),
        cost_estimate=cost(6 * ROWS * DEPTH * COLS, 14 * small),
    )(columns.reshape(DEPTH, COLS), depth_high, depth_low, numerator, denominator)
    return (sliding_acceleration, memory_change, heat_level_change, fluid_load_change)


def solution(mesh):
    plane = P("depth", "strike")
    block = P(None, "depth", "strike")
    return jax.shard_map(
        shards,
        mesh=mesh,
        in_specs=(plane,) * 7 + (block,) * 2,
        out_specs=(plane, plane, block, block),
        check_vma=False,
    )
```

```python
import math

import jax
import jax.numpy as jnp
import ml_dtypes
import numpy as np
from jax import lax
from jax.experimental import pallas as pl
from jax.experimental.pallas import tpu as pltpu
from jax.sharding import PartitionSpec as P

HEAT_GAIN = 0.05
HEAT_DIFFUSIVITY = 0.3
FLUID_DIFFUSIVITY = 0.45
FLUID_TOGGLE = 0.6
REF_FRICTION = 0.5
DAMPING = 0.5
RELAXATION = 0.2
ELASTIC = 4.0 / 3.0
HEAT_WIDTH = 4.0

DEPTH = 768
STRIKE = 8192
ROWS = 96
COLS = 256
POINTS = 32
DEPTH_PARTS = 8
STRIKE_PARTS = 32
LANES = 128
COARSE = STRIKE // LANES
CLASSES = COARSE // 2 + 1
PAIRS = 4
PAIR_MODES = DEPTH // PAIRS
PAIR_SIZE = 2 * STRIKE_PARTS
MODES = 3
SLOTS = 4
SPEC_ROWS = 112

F32 = jnp.float32
BF16 = jnp.bfloat16


def halves(table):
    high = table.astype(ml_dtypes.bfloat16)
    low = (table - high.astype(np.float64)).astype(ml_dtypes.bfloat16)
    return high, low


def depth_table():
    index = np.arange(DEPTH)
    angle = 2.0 * np.pi / DEPTH * (index[:, None] * index[None, :] % DEPTH)
    return np.cos(angle) + np.sin(angle)


def depth_tables():
    table = depth_table()
    forward = table.reshape(PAIRS, PAIR_MODES, DEPTH)
    inverse = table.reshape(DEPTH, PAIRS, PAIR_MODES).transpose(1, 0, 2)
    return forward, inverse


def coarse_tables():
    angle = 2.0 * np.pi / COARSE * (np.arange(CLASSES)[:, None] * np.arange(COARSE)[None, :] % COARSE)
    forward = np.zeros((2, SPEC_ROWS, COARSE, SLOTS))
    inverse = np.zeros((COARSE, SLOTS, 2, SPEC_ROWS))
    weight = np.where(np.arange(CLASSES) % (COARSE // 2) == 0, 1.0, 2.0)[:, None]
    for mode in range(MODES):
        at = np.arange(CLASSES) * MODES + mode
        forward[0, at, :, mode] = np.cos(angle)
        forward[1, at, :, mode] = -np.sin(angle)
        inverse[:, mode, 0, at] = (weight * np.cos(angle)).T
        inverse[:, mode, 1, at] = (-weight * np.sin(angle)).T
    return (
        forward.reshape(2 * SPEC_ROWS, COARSE * SLOTS),
        inverse.reshape(COARSE * SLOTS, 2 * SPEC_ROWS),
    )


def fine_tables():
    index = np.arange(LANES)
    angle = 2.0 * np.pi / LANES * (index[:, None] * index[None, :] % LANES)
    cosine, sine = np.cos(angle), np.sin(angle)
    forward = np.block([[cosine, -sine], [sine, cosine]])
    inverse = np.block([[cosine, sine], [-sine, cosine]])
    return forward, inverse


def class_tables():
    row = np.arange(SPEC_ROWS)
    k_one = np.minimum(row // MODES, CLASSES - 1)
    lane = np.arange(LANES)
    angle = 2.0 * np.pi / STRIKE * (k_one[:, None] * lane[None, :])
    wave = k_one[:, None] + COARSE * lane[None, :]
    strike_wave = 2.0 * np.pi / STRIKE * np.minimum(wave, STRIKE - wave)
    offset = np.broadcast_to((row % MODES * PAIR_SIZE)[:, None], (SPEC_ROWS, LANES))
    return tuple(
        np.asarray(table, np.float32)
        for table in (np.cos(angle), np.sin(angle), strike_wave * strike_wave, offset)
    )


def split(values):
    high = values.astype(BF16)
    return high, (values - high.astype(F32)).astype(BF16)


def mm(left, right):
    return jnp.dot(left, right, preferred_element_type=F32)


def table_first(high, low, values):
    v_high, v_low = split(values)
    return mm(high, v_high) + (mm(high, v_low) + mm(low, v_high))


def table_last(values, high, low):
    v_high, v_low = split(values)
    return mm(v_high, high) + (mm(v_low, high) + mm(v_high, low))


def field_kernel(
    speed_hbm,
    slip_hbm,
    table_high,
    table_low,
    out_ref,
    high_out,
    low_out,
    speed_ref,
    slip_ref,
    sems,
):
    pair = lax.axis_index("depth") // 2
    loads = [
        pltpu.make_async_copy(source, target, sems.at[at])
        for at, (source, target) in enumerate(
            (
                (speed_hbm, speed_ref),
                (slip_hbm, slip_ref),
                (table_high.at[pair], high_out),
                (table_low.at[pair], low_out),
            )
        )
    ]
    for load in loads:
        load.start()
    loads[0].wait()
    loads[1].wait()
    field = speed_ref[...] + RELAXATION * slip_ref[...]
    for part in range(DEPTH_PARTS):
        half = part % 2
        out_ref[part] = field[:, half * LANES : (half + 1) * LANES]
    loads[2].wait()
    loads[3].wait()


def depth_kernel(fields_ref, high_ref, low_ref, out_ref):
    modes = table_first(high_ref[...], low_ref[...], fields_ref[...])
    for slot in range(SLOTS):
        piece = jnp.zeros((PAIR_SIZE, LANES), F32)
        if slot < MODES:
            piece = modes[slot * PAIR_SIZE : (slot + 1) * PAIR_SIZE]
        out_ref[pl.ds(slot, PAIR_SIZE, stride=SLOTS), :] = piece


def strike_kernel(
    modes_ref,
    coarse_high,
    coarse_low,
    fine_high,
    fine_low,
    back_high,
    back_low,
    out_high,
    out_low,
    cos_ref,
    sin_ref,
    strike_square_ref,
    offset_ref,
    out_ref,
):
    cosine, sine = cos_ref[...], sin_ref[...]
    depth_pos = lax.axis_index("depth")
    base = depth_pos // 2 * PAIR_MODES + 2 * lax.axis_index("strike") + depth_pos % 2
    depth_index = offset_ref[...] + base.astype(F32)
    depth_wave = 2.0 * math.pi / DEPTH * jnp.minimum(depth_index, DEPTH - depth_index)
    depth_square = depth_wave * depth_wave
    strike_square = strike_square_ref[...]
    wave_square = strike_square + depth_square
    kernel = (
        (-0.5 / (DEPTH * STRIKE))
        * (strike_square * ELASTIC + depth_square)
        / jnp.sqrt(jnp.where(wave_square > 0, wave_square, 1.0))
    )
    coarse = table_first(coarse_high[...], coarse_low[...], modes_ref[...])
    real, imag = coarse[:SPEC_ROWS], coarse[SPEC_ROWS:]
    turned = jnp.concatenate([real * cosine + imag * sine, imag * cosine - real * sine], 1)
    spectrum = table_last(turned, fine_high[...], fine_low[...])
    spectrum = spectrum * jnp.concatenate([kernel, kernel], 1)
    back = table_last(spectrum, back_high[...], back_low[...])
    real, imag = back[:, :LANES], back[:, LANES:]
    turned = jnp.concatenate([real * cosine - imag * sine, imag * cosine + real * sine], 0)
    out_ref[...] = table_first(out_high[...], out_low[...], turned)


def depth_back_kernel(modes_ref, high_ref, low_ref, out_ref):
    pair = lax.axis_index("depth") // 2
    modes = jnp.concatenate(
        [modes_ref[pl.ds(slot, PAIR_SIZE, stride=SLOTS), :] for slot in range(MODES)], 0
    )
    out_ref[...] = table_first(high_ref[pair], low_ref[pair], modes)


def final_kernel(parts_ref, numerator_ref, denominator_ref, out_ref):
    for half in range(2):
        lanes = slice(half * LANES, (half + 1) * LANES)
        filtered = (parts_ref[half] + parts_ref[half + 2]) + (
            parts_ref[half + 4] + parts_ref[half + 6]
        )
        out_ref[:, lanes] = (filtered + numerator_ref[:, lanes]) / denominator_ref[:, lanes]


def stencil_kernel(
    speed_hbm,
    memory_hbm,
    clamping_hbm,
    effect_a_hbm,
    effect_b_hbm,
    ambient_hbm,
    heat_hbm,
    fluid_hbm,
    memory_hbm_out,
    numerator_out,
    denominator_out,
    heat_out,
    fluid_out,
    speed_ref,
    memory_ref,
    clamping_ref,
    effect_a_ref,
    effect_b_ref,
    ambient_ref,
    memory_out,
    heat_in,
    fluid_in,
    heat_change,
    fluid_change,
    in_sem,
    out_sem,
    plane_sem,
):
    plane_loads = [
        pltpu.make_async_copy(source, target, plane_sem.at[at])
        for at, (source, target) in enumerate(
            (
                (speed_hbm, speed_ref),
                (memory_hbm, memory_ref),
                (clamping_hbm, clamping_ref),
                (effect_a_hbm, effect_a_ref),
                (effect_b_hbm, effect_b_ref),
                (ambient_hbm, ambient_ref),
            )
        )
    ]
    memory_store = pltpu.make_async_copy(memory_out, memory_hbm_out, plane_sem.at[6])
    for load in plane_loads:
        load.start()

    def pieces(source, target, sems, which):
        return [
            pltpu.make_async_copy(
                source.at[:, pl.ds(part * BLOCK, BLOCK), :],
                target.at[:, pl.ds(part * BLOCK, BLOCK), :],
                sems.at[which, part],
            )
            for part in range(ROWS // BLOCK)
        ]

    heat_loads = pieces(heat_hbm, heat_in, in_sem, 0)
    fluid_loads = pieces(fluid_hbm, fluid_in, in_sem, 1)
    heat_stores = pieces(heat_change, heat_out, out_sem, 0)
    fluid_stores = pieces(fluid_change, fluid_out, out_sem, 1)
    for part in range(ROWS // BLOCK):
        fluid_loads[part].start()
        heat_loads[part].start()
    for load in plane_loads:
        load.wait()
    for part in range(ROWS // BLOCK):
        fluid_loads[part].wait()
        heat_loads[part].wait()
        for row in range(part * BLOCK, (part + 1) * BLOCK, 8):
            rows = slice(row, row + 8)
            speed, memory = speed_ref[rows], memory_ref[rows]
            effect_a, effect_b = effect_a_ref[rows], effect_b_ref[rows]
            ratio = memory / effect_a
            argument = 0.5 * speed * jnp.exp(ratio)
            friction = effect_a * jnp.log(argument + jnp.sqrt(argument * argument + 1.0))
            root_term = jnp.sqrt(4.0 * jnp.exp(-2.0 * ratio) + speed * speed)
            effective = clamping_ref[rows] - fluid_in[0, rows]
            traction = effective * friction
            power = HEAT_GAIN * traction * speed
            memory_change = effect_b * (jnp.exp((REF_FRICTION - memory) / effect_b) - speed)
            memory_out[rows] = memory_change
            heat, fluid = heat_in[0, rows], fluid_in[0, rows]
            heat_above, fluid_above = heat_in[1, rows], fluid_in[1, rows]
            heat_below, fluid_below = heat_above, fluid_above
            for point in range(POINTS):
                bent = heat_below - 2.0 * heat
                pressed = fluid_below - 2.0 * fluid
                if point + 1 < POINTS:
                    bent = bent + heat_above
                    pressed = pressed + fluid_above
                warmed = HEAT_DIFFUSIVITY * bent + math.exp(-((point / HEAT_WIDTH) ** 2)) * power
                pressed = FLUID_DIFFUSIVITY * pressed + FLUID_TOGGLE * warmed
                heat_change[point, rows] = warmed
                fluid_change[point, rows] = pressed
                if point == 0:
                    extra = (
                        friction * pressed - effective * (speed / root_term) * memory_change
                    )
                    numerator_out[rows] = extra + RELAXATION * (
                        ambient_ref[rows] - DAMPING * speed - traction
                    )
                    denominator_out[rows] = effective * effect_a / root_term + DAMPING
                heat_below, fluid_below = heat, fluid
                heat, fluid = heat_above, fluid_above
                if point + 2 < POINTS:
                    heat_above, fluid_above = heat_in[point + 2, rows], fluid_in[point + 2, rows]
        heat_stores[part].start()
        fluid_stores[part].start()
    memory_store.start()
    memory_store.wait()
    for part in range(ROWS // BLOCK):
        heat_stores[part].wait()
        fluid_stores[part].wait()


def whole(count):
    return [pl.BlockSpec(memory_space=pltpu.VMEM)] * count


def anywhere(count):
    return [pl.BlockSpec(memory_space=pltpu.HBM)] * count


def in_hbm(*arrays):
    return [pltpu.with_memory_space_constraint(jnp.asarray(x), pltpu.HBM) for x in arrays]


def cost(flops, moved):
    return pl.CostEstimate(flops=flops, bytes_accessed=moved, transcendentals=0)


def shape(*dims):
    return jax.ShapeDtypeStruct(dims, F32)


BLOCK = 16


def grant(mebibytes):
    return pltpu.CompilerParams(vmem_limit_bytes=mebibytes * 1024 * 1024)


def shards(
    sliding_speed,
    offset_displacement,
    contact_memory,
    clamping_traction,
    instant_effect_a,
    healing_effect_b,
    ambient_traction,
    heat_level,
    fluid_load,
):
    depth_forward, depth_inverse = depth_tables()
    coarse_forward, coarse_inverse = coarse_tables()
    fine_forward, fine_inverse = fine_tables()
    small = ROWS * COLS * 4
    groups = [
        [(2 * pair + half) * STRIKE_PARTS + part for part in range(STRIKE_PARTS) for half in (0, 1)]
        for pair in range(PAIRS)
    ]

    def over_depth(pieces):
        return lax.all_to_all(pieces, "depth", split_axis=0, concat_axis=0)

    def over_pair(pieces):
        pieces = pieces.reshape(PAIR_SIZE, SLOTS, LANES)
        moved = lax.all_to_all(
            pieces, ("depth", "strike"), split_axis=0, concat_axis=0, axis_index_groups=groups
        )
        return moved.reshape(PAIR_SIZE * SLOTS, LANES)

    sent, depth_high, depth_low = pl.pallas_call(
        field_kernel,
        out_shape=(
            shape(DEPTH_PARTS, ROWS, LANES),
            pltpu.VMEM((PAIR_MODES, DEPTH), BF16),
            pltpu.VMEM((PAIR_MODES, DEPTH), BF16),
        ),
        in_specs=[pl.BlockSpec(memory_space=pltpu.HBM)] * 4,
        out_specs=whole(3),
        scratch_shapes=[pltpu.VMEM((ROWS, COLS), F32)] * 2 + [pltpu.SemaphoreType.DMA((4,))],
        compiler_params=grant(4),
        cost_estimate=cost(2 * ROWS * COLS, 12 * small),
    )(*in_hbm(sliding_speed, offset_displacement, *halves(depth_forward)))
    columns = over_depth(sent)

    modes = pl.pallas_call(
        depth_kernel,
        out_shape=shape(PAIR_SIZE * SLOTS, LANES),
        in_specs=whole(3),
        out_specs=pl.BlockSpec(memory_space=pltpu.VMEM),
        compiler_params=grant(10),
        cost_estimate=cost(6 * PAIR_MODES * DEPTH * LANES, 12 * small),
    )(columns.reshape(DEPTH, LANES), depth_high, depth_low)

    filtered = pl.pallas_call(
        strike_kernel,
        out_shape=shape(PAIR_SIZE * SLOTS, LANES),
        in_specs=whole(13),
        out_specs=pl.BlockSpec(memory_space=pltpu.VMEM),
        compiler_params=grant(6),
        cost_estimate=cost(6 * 4 * 256 * 256 * LANES, 15 * small),
    )(
        over_pair(modes),
        *halves(coarse_forward),
        *halves(fine_forward),
        *halves(fine_inverse),
        *halves(coarse_inverse),
        *class_tables(),
    )

    sent = pl.pallas_call(
        depth_back_kernel,
        out_shape=shape(DEPTH, LANES),
        in_specs=whole(3),
        out_specs=pl.BlockSpec(memory_space=pltpu.VMEM),
        compiler_params=grant(10),
        cost_estimate=cost(6 * PAIR_MODES * DEPTH * LANES, 12 * small),
    )(over_pair(filtered), *halves(depth_inverse))
    parts = over_depth(sent.reshape(DEPTH_PARTS, ROWS, LANES))

    memory_change, numerator, denominator, heat_level_change, fluid_load_change = pl.pallas_call(
        stencil_kernel,
        out_shape=(
            shape(ROWS, COLS),
            pltpu.VMEM((ROWS, COLS), F32),
            pltpu.VMEM((ROWS, COLS), F32),
            shape(POINTS, ROWS, COLS),
            shape(POINTS, ROWS, COLS),
        ),
        in_specs=anywhere(8),
        out_specs=anywhere(1) + whole(2) + anywhere(2),
        scratch_shapes=[pltpu.VMEM((ROWS, COLS), F32)] * 7
        + [pltpu.VMEM((POINTS, ROWS, COLS), F32)] * 4
        + [pltpu.SemaphoreType.DMA((2, ROWS // BLOCK))] * 2
        + [pltpu.SemaphoreType.DMA((7,))],
        compiler_params=grant(20),
        cost_estimate=cost(18 * POINTS * ROWS * COLS, 137 * small),
    )(
        *in_hbm(
            sliding_speed,
            contact_memory,
            clamping_traction,
            instant_effect_a,
            healing_effect_b,
            ambient_traction,
            heat_level,
            fluid_load,
        )
    )

    sliding_acceleration = pl.pallas_call(
        final_kernel,
        out_shape=shape(ROWS, COLS),
        in_specs=whole(3),
        out_specs=pl.BlockSpec(memory_space=pltpu.VMEM),
        compiler_params=grant(4),
        cost_estimate=cost(5 * ROWS * COLS, 7 * small),
    )(parts, numerator, denominator)
    return (sliding_acceleration, memory_change, heat_level_change, fluid_load_change)


def solution(mesh):
    plane = P("depth", "strike")
    block = P(None, "depth", "strike")
    return jax.shard_map(
        shards,
        mesh=mesh,
        in_specs=(plane,) * 7 + (block,) * 2,
        out_specs=(plane, plane, block, block),
        check_vma=False,
    )
```

```python
import math

import jax
import jax.numpy as jnp
import ml_dtypes
import numpy as np
from jax import lax
from jax.experimental import pallas as pl
from jax.experimental.pallas import tpu as pltpu
from jax.sharding import PartitionSpec as P

HEAT_GAIN = 0.05
HEAT_DIFFUSIVITY = 0.3
FLUID_DIFFUSIVITY = 0.45
FLUID_TOGGLE = 0.6
REF_FRICTION = 0.5
DAMPING = 0.5
RELAXATION = 0.2
ELASTIC = 4.0 / 3.0
HEAT_WIDTH = 4.0

DEPTH = 768
STRIKE = 8192
ROWS = 96
COLS = 256
POINTS = 32
DEPTH_PARTS = 8
STRIKE_PARTS = 32
LANES = 128
COARSE = STRIKE // LANES
CLASSES = COARSE // 2 + 1
PAIRS = 4
PAIR_MODES = DEPTH // PAIRS
PAIR_SIZE = 2 * STRIKE_PARTS
MODES = 3
PAIR_ROWS = PAIR_SIZE * MODES
SPEC_ROWS = 112

F32 = jnp.float32
BF16 = jnp.bfloat16


def halves(table):
    high = table.astype(ml_dtypes.bfloat16)
    low = (table - high.astype(np.float64)).astype(ml_dtypes.bfloat16)
    return high, low


def depth_table():
    index = np.arange(DEPTH)
    angle = 2.0 * np.pi / DEPTH * (index[:, None] * index[None, :] % DEPTH)
    return np.cos(angle) + np.sin(angle)


def depth_tables():
    table = depth_table()
    forward = table.reshape(PAIRS, PAIR_MODES, DEPTH)
    inverse = table.reshape(DEPTH, PAIRS, PAIR_MODES).transpose(1, 0, 2)
    return forward, inverse


def coarse_tables():
    angle = 2.0 * np.pi / COARSE * (np.arange(CLASSES)[:, None] * np.arange(COARSE)[None, :] % COARSE)
    forward = np.zeros((2, SPEC_ROWS, COARSE, MODES))
    inverse = np.zeros((COARSE, MODES, 2, SPEC_ROWS))
    weight = np.where(np.arange(CLASSES) % (COARSE // 2) == 0, 1.0, 2.0)[:, None]
    for mode in range(MODES):
        at = np.arange(CLASSES) * MODES + mode
        forward[0, at, :, mode] = np.cos(angle)
        forward[1, at, :, mode] = -np.sin(angle)
        inverse[:, mode, 0, at] = (weight * np.cos(angle)).T
        inverse[:, mode, 1, at] = (-weight * np.sin(angle)).T
    piece = np.arange(PAIR_SIZE)
    order = 2 * (piece % STRIKE_PARTS) + piece // STRIKE_PARTS
    return (
        forward[:, :, order].reshape(2 * SPEC_ROWS, PAIR_ROWS),
        inverse[order].reshape(PAIR_ROWS, 2 * SPEC_ROWS),
    )


def fine_tables():
    index = np.arange(LANES)
    angle = 2.0 * np.pi / LANES * (index[:, None] * index[None, :] % LANES)
    cosine, sine = np.cos(angle), np.sin(angle)
    forward = np.block([[cosine, -sine], [sine, cosine]])
    inverse = np.block([[cosine, sine], [-sine, cosine]])
    return forward, inverse


def class_tables():
    row = np.arange(SPEC_ROWS)
    k_one = np.minimum(row // MODES, CLASSES - 1)
    lane = np.arange(LANES)
    angle = 2.0 * np.pi / STRIKE * (k_one[:, None] * lane[None, :])
    wave = k_one[:, None] + COARSE * lane[None, :]
    strike_wave = 2.0 * np.pi / STRIKE * np.minimum(wave, STRIKE - wave)
    offset = np.broadcast_to((row % MODES * PAIR_SIZE)[:, None], (SPEC_ROWS, LANES))
    return tuple(
        np.asarray(table, np.float32)
        for table in (np.cos(angle), np.sin(angle), strike_wave * strike_wave, offset)
    )


def split(values):
    high = values.astype(BF16)
    return high, (values - high.astype(F32)).astype(BF16)


def mm(left, right):
    return jnp.dot(left, right, preferred_element_type=F32)


def table_first(high, low, values):
    v_high, v_low = split(values)
    return mm(high, v_high) + (mm(high, v_low) + mm(low, v_high))


def table_last(values, high, low):
    v_high, v_low = split(values)
    return mm(v_high, high) + (mm(v_low, high) + mm(v_high, low))


def field_kernel(
    speed_hbm,
    slip_hbm,
    table_high,
    table_low,
    out_ref,
    high_out,
    low_out,
    speed_ref,
    slip_ref,
    sems,
):
    pair = lax.axis_index("depth") // 2
    loads = [
        pltpu.make_async_copy(source, target, sems.at[at])
        for at, (source, target) in enumerate(
            (
                (speed_hbm, speed_ref),
                (slip_hbm, slip_ref),
                (table_high.at[pair], high_out),
                (table_low.at[pair], low_out),
            )
        )
    ]
    for load in loads:
        load.start()
    loads[0].wait()
    loads[1].wait()
    field = speed_ref[...] + RELAXATION * slip_ref[...]
    for part in range(DEPTH_PARTS):
        half = part % 2
        out_ref[part] = field[:, half * LANES : (half + 1) * LANES]
    loads[2].wait()
    loads[3].wait()


def depth_kernel(fields_ref, high_ref, low_ref, out_ref):
    modes = table_first(high_ref[...], low_ref[...], fields_ref[...])
    for slot in range(MODES):
        out_ref[pl.ds(slot, PAIR_SIZE, stride=MODES), :] = modes[
            slot * PAIR_SIZE : (slot + 1) * PAIR_SIZE
        ]


def strike_kernel(
    modes_ref,
    coarse_high,
    coarse_low,
    fine_high,
    fine_low,
    back_high,
    back_low,
    out_high,
    out_low,
    cos_ref,
    sin_ref,
    strike_square_ref,
    offset_ref,
    out_ref,
):
    cosine, sine = cos_ref[...], sin_ref[...]
    depth_pos = lax.axis_index("depth")
    base = (
        depth_pos // 2 * PAIR_MODES + depth_pos % 2 * STRIKE_PARTS + lax.axis_index("strike")
    )
    depth_index = offset_ref[...] + base.astype(F32)
    depth_wave = 2.0 * math.pi / DEPTH * jnp.minimum(depth_index, DEPTH - depth_index)
    depth_square = depth_wave * depth_wave
    strike_square = strike_square_ref[...]
    wave_square = strike_square + depth_square
    kernel = (
        (-0.5 / (DEPTH * STRIKE))
        * (strike_square * ELASTIC + depth_square)
        / jnp.sqrt(jnp.where(wave_square > 0, wave_square, 1.0))
    )
    coarse = table_first(coarse_high[...], coarse_low[...], modes_ref[...])
    real, imag = coarse[:SPEC_ROWS], coarse[SPEC_ROWS:]
    turned = jnp.concatenate([real * cosine + imag * sine, imag * cosine - real * sine], 1)
    spectrum = table_last(turned, fine_high[...], fine_low[...])
    spectrum = spectrum * jnp.concatenate([kernel, kernel], 1)
    back = table_last(spectrum, back_high[...], back_low[...])
    real, imag = back[:, :LANES], back[:, LANES:]
    turned = jnp.concatenate([real * cosine - imag * sine, imag * cosine + real * sine], 0)
    out_ref[...] = table_first(out_high[...], out_low[...], turned)


def depth_back_kernel(modes_ref, high_ref, low_ref, out_ref):
    pair = lax.axis_index("depth") // 2
    modes = jnp.concatenate(
        [modes_ref[pl.ds(slot, PAIR_SIZE, stride=MODES), :] for slot in range(MODES)], 0
    )
    out_ref[...] = table_first(high_ref[pair], low_ref[pair], modes)


def final_kernel(parts_ref, numerator_ref, denominator_ref, out_ref):
    for half in range(2):
        lanes = slice(half * LANES, (half + 1) * LANES)
        filtered = (parts_ref[half] + parts_ref[half + 2]) + (
            parts_ref[half + 4] + parts_ref[half + 6]
        )
        out_ref[:, lanes] = (filtered + numerator_ref[:, lanes]) / denominator_ref[:, lanes]


def stencil_kernel(
    speed_hbm,
    memory_hbm,
    clamping_hbm,
    effect_a_hbm,
    effect_b_hbm,
    ambient_hbm,
    heat_hbm,
    fluid_hbm,
    memory_hbm_out,
    numerator_out,
    denominator_out,
    heat_out,
    fluid_out,
    speed_ref,
    memory_ref,
    clamping_ref,
    effect_a_ref,
    effect_b_ref,
    ambient_ref,
    memory_out,
    heat_in,
    fluid_in,
    heat_change,
    fluid_change,
    in_sem,
    out_sem,
    plane_sem,
):
    plane_loads = [
        pltpu.make_async_copy(source, target, plane_sem.at[at])
        for at, (source, target) in enumerate(
            (
                (speed_hbm, speed_ref),
                (memory_hbm, memory_ref),
                (clamping_hbm, clamping_ref),
                (effect_a_hbm, effect_a_ref),
                (effect_b_hbm, effect_b_ref),
                (ambient_hbm, ambient_ref),
            )
        )
    ]
    memory_store = pltpu.make_async_copy(memory_out, memory_hbm_out, plane_sem.at[6])
    for load in plane_loads:
        load.start()

    def pieces(source, target, sems, which):
        return [
            pltpu.make_async_copy(
                source.at[:, pl.ds(part * BLOCK, BLOCK), :],
                target.at[:, pl.ds(part * BLOCK, BLOCK), :],
                sems.at[which, part],
            )
            for part in range(ROWS // BLOCK)
        ]

    heat_loads = pieces(heat_hbm, heat_in, in_sem, 0)
    fluid_loads = pieces(fluid_hbm, fluid_in, in_sem, 1)
    heat_stores = pieces(heat_change, heat_out, out_sem, 0)
    fluid_stores = pieces(fluid_change, fluid_out, out_sem, 1)
    for part in range(ROWS // BLOCK):
        fluid_loads[part].start()
        heat_loads[part].start()
    for load in plane_loads:
        load.wait()
    for part in range(ROWS // BLOCK):
        fluid_loads[part].wait()
        heat_loads[part].wait()
        for row in range(part * BLOCK, (part + 1) * BLOCK, 8):
            rows = slice(row, row + 8)
            speed, memory = speed_ref[rows], memory_ref[rows]
            effect_a, effect_b = effect_a_ref[rows], effect_b_ref[rows]
            ratio = memory / effect_a
            argument = 0.5 * speed * jnp.exp(ratio)
            friction = effect_a * jnp.log(argument + jnp.sqrt(argument * argument + 1.0))
            root_term = jnp.sqrt(4.0 * jnp.exp(-2.0 * ratio) + speed * speed)
            effective = clamping_ref[rows] - fluid_in[0, rows]
            traction = effective * friction
            power = HEAT_GAIN * traction * speed
            memory_change = effect_b * (jnp.exp((REF_FRICTION - memory) / effect_b) - speed)
            memory_out[rows] = memory_change
            heat, fluid = heat_in[0, rows], fluid_in[0, rows]
            heat_above, fluid_above = heat_in[1, rows], fluid_in[1, rows]
            heat_below, fluid_below = heat_above, fluid_above
            for point in range(POINTS):
                bent = heat_below - 2.0 * heat
                pressed = fluid_below - 2.0 * fluid
                if point + 1 < POINTS:
                    bent = bent + heat_above
                    pressed = pressed + fluid_above
                warmed = HEAT_DIFFUSIVITY * bent + math.exp(-((point / HEAT_WIDTH) ** 2)) * power
                pressed = FLUID_DIFFUSIVITY * pressed + FLUID_TOGGLE * warmed
                heat_change[point, rows] = warmed
                fluid_change[point, rows] = pressed
                if point == 0:
                    extra = (
                        friction * pressed - effective * (speed / root_term) * memory_change
                    )
                    numerator_out[rows] = extra + RELAXATION * (
                        ambient_ref[rows] - DAMPING * speed - traction
                    )
                    denominator_out[rows] = effective * effect_a / root_term + DAMPING
                heat_below, fluid_below = heat, fluid
                heat, fluid = heat_above, fluid_above
                if point + 2 < POINTS:
                    heat_above, fluid_above = heat_in[point + 2, rows], fluid_in[point + 2, rows]
        heat_stores[part].start()
        fluid_stores[part].start()
    memory_store.start()
    memory_store.wait()
    for part in range(ROWS // BLOCK):
        heat_stores[part].wait()
        fluid_stores[part].wait()


def whole(count):
    return [pl.BlockSpec(memory_space=pltpu.VMEM)] * count


def anywhere(count):
    return [pl.BlockSpec(memory_space=pltpu.HBM)] * count


def in_hbm(*arrays):
    return [pltpu.with_memory_space_constraint(jnp.asarray(x), pltpu.HBM) for x in arrays]


def cost(flops, moved):
    return pl.CostEstimate(flops=flops, bytes_accessed=moved, transcendentals=0)


def shape(*dims):
    return jax.ShapeDtypeStruct(dims, F32)


BLOCK = 16


def grant(mebibytes):
    return pltpu.CompilerParams(vmem_limit_bytes=mebibytes * 1024 * 1024)


def shards(
    sliding_speed,
    offset_displacement,
    contact_memory,
    clamping_traction,
    instant_effect_a,
    healing_effect_b,
    ambient_traction,
    heat_level,
    fluid_load,
):
    depth_forward, depth_inverse = depth_tables()
    coarse_forward, coarse_inverse = coarse_tables()
    fine_forward, fine_inverse = fine_tables()
    small = ROWS * COLS * 4
    groups = [
        [(2 * pair + half) * STRIKE_PARTS + part for half in (0, 1) for part in range(STRIKE_PARTS)]
        for pair in range(PAIRS)
    ]

    def over_depth(pieces):
        return lax.all_to_all(pieces, "depth", split_axis=0, concat_axis=0)

    def over_pair(pieces):
        pieces = pieces.reshape(PAIR_SIZE, 1, MODES * LANES)
        moved = lax.all_to_all(
            pieces, ("depth", "strike"), split_axis=0, concat_axis=0, axis_index_groups=groups
        )
        return moved.reshape(PAIR_ROWS, LANES)

    sent, depth_high, depth_low = pl.pallas_call(
        field_kernel,
        out_shape=(
            shape(DEPTH_PARTS, ROWS, LANES),
            pltpu.VMEM((PAIR_MODES, DEPTH), BF16),
            pltpu.VMEM((PAIR_MODES, DEPTH), BF16),
        ),
        in_specs=[pl.BlockSpec(memory_space=pltpu.HBM)] * 4,
        out_specs=whole(3),
        scratch_shapes=[pltpu.VMEM((ROWS, COLS), F32)] * 2 + [pltpu.SemaphoreType.DMA((4,))],
        compiler_params=grant(4),
        cost_estimate=cost(2 * ROWS * COLS, 12 * small),
    )(*in_hbm(sliding_speed, offset_displacement, *halves(depth_forward)))
    columns = over_depth(sent)

    modes = pl.pallas_call(
        depth_kernel,
        out_shape=shape(PAIR_ROWS, LANES),
        in_specs=whole(3),
        out_specs=pl.BlockSpec(memory_space=pltpu.VMEM),
        compiler_params=grant(10),
        cost_estimate=cost(6 * PAIR_MODES * DEPTH * LANES, 12 * small),
    )(columns.reshape(DEPTH, LANES), depth_high, depth_low)

    filtered = pl.pallas_call(
        strike_kernel,
        out_shape=shape(PAIR_ROWS, LANES),
        in_specs=whole(13),
        out_specs=pl.BlockSpec(memory_space=pltpu.VMEM),
        compiler_params=grant(6),
        cost_estimate=cost(6 * 4 * 256 * 256 * LANES, 15 * small),
    )(
        over_pair(modes),
        *halves(coarse_forward),
        *halves(fine_forward),
        *halves(fine_inverse),
        *halves(coarse_inverse),
        *class_tables(),
    )

    sent = pl.pallas_call(
        depth_back_kernel,
        out_shape=shape(DEPTH, LANES),
        in_specs=whole(3),
        out_specs=pl.BlockSpec(memory_space=pltpu.VMEM),
        compiler_params=grant(10),
        cost_estimate=cost(6 * PAIR_MODES * DEPTH * LANES, 12 * small),
    )(over_pair(filtered), *halves(depth_inverse))
    parts = over_depth(sent.reshape(DEPTH_PARTS, ROWS, LANES))

    memory_change, numerator, denominator, heat_level_change, fluid_load_change = pl.pallas_call(
        stencil_kernel,
        out_shape=(
            shape(ROWS, COLS),
            pltpu.VMEM((ROWS, COLS), F32),
            pltpu.VMEM((ROWS, COLS), F32),
            shape(POINTS, ROWS, COLS),
            shape(POINTS, ROWS, COLS),
        ),
        in_specs=anywhere(8),
        out_specs=anywhere(1) + whole(2) + anywhere(2),
        scratch_shapes=[pltpu.VMEM((ROWS, COLS), F32)] * 7
        + [pltpu.VMEM((POINTS, ROWS, COLS), F32)] * 4
        + [pltpu.SemaphoreType.DMA((2, ROWS // BLOCK))] * 2
        + [pltpu.SemaphoreType.DMA((7,))],
        compiler_params=grant(20),
        cost_estimate=cost(18 * POINTS * ROWS * COLS, 137 * small),
    )(
        *in_hbm(
            sliding_speed,
            contact_memory,
            clamping_traction,
            instant_effect_a,
            healing_effect_b,
            ambient_traction,
            heat_level,
            fluid_load,
        )
    )

    sliding_acceleration = pl.pallas_call(
        final_kernel,
        out_shape=shape(ROWS, COLS),
        in_specs=whole(3),
        out_specs=pl.BlockSpec(memory_space=pltpu.VMEM),
        compiler_params=grant(4),
        cost_estimate=cost(5 * ROWS * COLS, 7 * small),
    )(parts, numerator, denominator)
    return (sliding_acceleration, memory_change, heat_level_change, fluid_load_change)


def solution(mesh):
    plane = P("depth", "strike")
    block = P(None, "depth", "strike")
    return jax.shard_map(
        shards,
        mesh=mesh,
        in_specs=(plane,) * 7 + (block,) * 2,
        out_specs=(plane, plane, block, block),
        check_vma=False,
    )
```

```python
import math

import jax
import jax.numpy as jnp
import ml_dtypes
import numpy as np
from jax import lax
from jax.experimental import pallas as pl
from jax.experimental.pallas import tpu as pltpu
from jax.sharding import PartitionSpec as P

HEAT_GAIN = 0.05
HEAT_DIFFUSIVITY = 0.3
FLUID_DIFFUSIVITY = 0.45
FLUID_TOGGLE = 0.6
REF_FRICTION = 0.5
DAMPING = 0.5
RELAXATION = 0.2
ELASTIC = 4.0 / 3.0
HEAT_WIDTH = 4.0

DEPTH = 768
STRIKE = 8192
ROWS = 96
COLS = 256
POINTS = 32
DEPTH_PARTS = 8
STRIKE_PARTS = 32
LANES = 128
COARSE = STRIKE // LANES
CLASSES = COARSE // 2 + 1
PAIRS = 4
PAIR_MODES = DEPTH // PAIRS
PAIR_SIZE = 2 * STRIKE_PARTS
MODES = 3
PAIR_ROWS = PAIR_SIZE * MODES
TABLE_CHUNKS = 1
BACK_CHUNKS = 6
SPEC_ROWS = 112

ORDER = "hxzc"
SIZES = {"h": 2, "x": 2, "z": 8, "c": 2}
WEIGHTS = {name: math.prod(SIZES[k] for k in ORDER[at + 1 :]) for at, name in enumerate(ORDER)}
DIGITS = [
    {name: place // WEIGHTS[name] % SIZES[name] for name in ORDER} for place in range(PAIR_SIZE)
]
PIECES = [(16 * d["x"] + 2 * d["z"] + d["c"], d["h"]) for d in DIGITS]

F32 = jnp.float32
BF16 = jnp.bfloat16


def halves(table):
    high = table.astype(ml_dtypes.bfloat16)
    low = (table - high.astype(np.float64)).astype(ml_dtypes.bfloat16)
    return np.concatenate([high, low], -2)


def depth_table():
    index = np.arange(DEPTH)
    angle = 2.0 * np.pi / DEPTH * (index[:, None] * index[None, :] % DEPTH)
    return np.cos(angle) + np.sin(angle)


def coarse_tables():
    angle = 2.0 * np.pi / COARSE * (np.arange(CLASSES)[:, None] * np.arange(COARSE)[None, :] % COARSE)
    forward = np.zeros((2, SPEC_ROWS, COARSE, MODES))
    inverse = np.zeros((COARSE, MODES, 2, SPEC_ROWS))
    weight = np.where(np.arange(CLASSES) % (COARSE // 2) == 0, 1.0, 2.0)[:, None]
    for mode in range(MODES):
        at = np.arange(CLASSES) * MODES + mode
        forward[0, at, :, mode] = np.cos(angle)
        forward[1, at, :, mode] = -np.sin(angle)
        inverse[:, mode, 0, at] = (weight * np.cos(angle)).T
        inverse[:, mode, 1, at] = (-weight * np.sin(angle)).T
    order = [2 * part + half for part, half in PIECES]
    return (
        forward[:, :, order].reshape(2 * SPEC_ROWS, PAIR_ROWS),
        inverse[order].reshape(PAIR_ROWS, 2 * SPEC_ROWS),
    )


def fine_tables():
    index = np.arange(LANES)
    angle = 2.0 * np.pi / LANES * (index[:, None] * index[None, :] % LANES)
    cosine, sine = np.cos(angle), np.sin(angle)
    forward = np.block([[cosine, -sine], [sine, cosine]])
    inverse = np.block([[cosine, sine], [-sine, cosine]])
    return forward, inverse


def class_tables():
    row = np.arange(SPEC_ROWS)
    k_one = np.minimum(row // MODES, CLASSES - 1)
    lane = np.arange(LANES)
    angle = 2.0 * np.pi / STRIKE * (k_one[:, None] * lane[None, :])
    wave = k_one[:, None] + COARSE * lane[None, :]
    strike_wave = 2.0 * np.pi / STRIKE * np.minimum(wave, STRIKE - wave)
    offset = np.broadcast_to((row % MODES * PAIR_SIZE)[:, None], (SPEC_ROWS, LANES))
    tables = (np.cos(angle), np.sin(angle), strike_wave * strike_wave, offset)
    return np.stack(tables).astype(np.float32)


def split(values):
    high = values.astype(BF16)
    return high, (values - high.astype(F32)).astype(BF16)


def mm(left, right):
    return jnp.dot(left, right, preferred_element_type=F32)


def table_first(table, values):
    rows = table.shape[0] // 2
    v_high, v_low = split(values)
    both = mm(table, v_high)
    return both[:rows] + (both[rows:] + mm(table[:rows], v_low))


def table_last(values, table):
    rows, depth = values.shape
    v_high, v_low = split(values)
    both = mm(jnp.concatenate([v_high, v_low], 0), table[:depth])
    return both[:rows] + (both[rows:] + mm(v_high, table[depth:]))


def table_turned(table, values):
    rows = table.shape[0] // 2
    v_high, v_low = split(values)

    def product(left, right):
        return lax.dot_general(
            left, right, (((0,), (0,)), ((), ())), preferred_element_type=F32
        )

    return product(table[:rows], v_high) + (
        product(table[:rows], v_low) + product(table[rows:], v_high)
    )


def field_kernel(speed_hbm, slip_hbm, table_hbm, out_ref, table_out, speed_ref, slip_ref, sems):
    pair = lax.axis_index("depth") // 2
    loads = [
        pltpu.make_async_copy(source, target, sems.at[at])
        for at, (source, target) in enumerate(((speed_hbm, speed_ref), (slip_hbm, slip_ref)))
    ]
    chunk = 2 * PAIR_MODES // TABLE_CHUNKS
    for part in range(TABLE_CHUNKS):
        rows = pl.ds(part * chunk, chunk)
        loads.append(
            pltpu.make_async_copy(
                table_hbm.at[pair, rows], table_out.at[rows], sems.at[2 + part]
            )
        )
    for load in loads:
        load.start()
    loads[0].wait()
    loads[1].wait()
    field = speed_ref[...] + RELAXATION * slip_ref[...]
    for part in range(DEPTH_PARTS):
        half = part % 2
        out_ref[part] = field[:, half * LANES : (half + 1) * LANES]
    for load in loads[2:]:
        load.wait()


def depth_kernel(fields_ref, table_ref, out_ref):
    modes = table_first(table_ref[...], fields_ref[...])
    for slot in range(MODES):
        out_ref[pl.ds(slot, PAIR_SIZE, stride=MODES), :] = modes[
            slot * PAIR_SIZE : (slot + 1) * PAIR_SIZE
        ]


def strike_kernel(modes_ref, coarse_ref, fine_ref, back_ref, out_table, class_ref, out_ref):
    cosine, sine = class_ref[0], class_ref[1]
    depth_pos, strike_pos = lax.axis_index("depth"), lax.axis_index("strike")
    place = (
        depth_pos % 2 * WEIGHTS["h"]
        + strike_pos // 16 * WEIGHTS["x"]
        + strike_pos // 2 % 8 * WEIGHTS["z"]
        + strike_pos % 2 * WEIGHTS["c"]
    )
    base = depth_pos // 2 * PAIR_MODES + place
    depth_index = class_ref[3] + base.astype(F32)
    depth_wave = 2.0 * math.pi / DEPTH * jnp.minimum(depth_index, DEPTH - depth_index)
    depth_square = depth_wave * depth_wave
    strike_square = class_ref[2]
    wave_square = strike_square + depth_square
    kernel = (
        (-0.5 / (DEPTH * STRIKE))
        * (strike_square * ELASTIC + depth_square)
        / jnp.sqrt(jnp.where(wave_square > 0, wave_square, 1.0))
    )
    coarse = table_first(coarse_ref[...], modes_ref[...])
    real, imag = coarse[:SPEC_ROWS], coarse[SPEC_ROWS:]
    turned = jnp.concatenate([real * cosine + imag * sine, imag * cosine - real * sine], 1)
    spectrum = table_last(turned, fine_ref[...])
    spectrum = spectrum * jnp.concatenate([kernel, kernel], 1)
    back = table_last(spectrum, back_ref[...])
    real, imag = back[:, :LANES], back[:, LANES:]
    turned = jnp.concatenate([real * cosine - imag * sine, imag * cosine + real * sine], 0)
    out_ref[...] = table_first(out_table[...], turned)


def depth_back_kernel(modes_ref, table_ref, out_hbm, out_ref, sems):
    modes = jnp.concatenate(
        [modes_ref[pl.ds(slot, PAIR_SIZE, stride=MODES), :] for slot in range(MODES)], 0
    )
    stores = []
    for part in range(BACK_CHUNKS):
        rows = slice(part * DEPTH // BACK_CHUNKS, (part + 1) * DEPTH // BACK_CHUNKS)
        out_ref[rows] = table_turned(table_ref[:, rows], modes)
        stores.append(pltpu.make_async_copy(out_ref.at[rows], out_hbm.at[rows], sems.at[part]))
        stores[-1].start()
    for store in stores:
        store.wait()


def final_kernel(parts_ref, numerator_ref, denominator_ref, out_ref):
    for half in range(2):
        lanes = slice(half * LANES, (half + 1) * LANES)
        filtered = (parts_ref[half] + parts_ref[half + 2]) + (
            parts_ref[half + 4] + parts_ref[half + 6]
        )
        out_ref[:, lanes] = (filtered + numerator_ref[:, lanes]) / denominator_ref[:, lanes]


def stencil_kernel(
    speed_hbm,
    memory_hbm,
    clamping_hbm,
    effect_a_hbm,
    effect_b_hbm,
    ambient_hbm,
    heat_hbm,
    fluid_hbm,
    memory_hbm_out,
    numerator_out,
    denominator_out,
    heat_out,
    fluid_out,
    speed_ref,
    memory_ref,
    clamping_ref,
    effect_a_ref,
    effect_b_ref,
    ambient_ref,
    memory_out,
    heat_in,
    fluid_in,
    heat_change,
    fluid_change,
    in_sem,
    out_sem,
    plane_sem,
):
    plane_loads = [
        pltpu.make_async_copy(source, target, plane_sem.at[at])
        for at, (source, target) in enumerate(
            (
                (speed_hbm, speed_ref),
                (memory_hbm, memory_ref),
                (clamping_hbm, clamping_ref),
                (effect_a_hbm, effect_a_ref),
                (effect_b_hbm, effect_b_ref),
                (ambient_hbm, ambient_ref),
            )
        )
    ]
    memory_store = pltpu.make_async_copy(memory_out, memory_hbm_out, plane_sem.at[6])
    for load in plane_loads:
        load.start()

    def pieces(source, target, sems, which):
        return [
            pltpu.make_async_copy(
                source.at[:, pl.ds(part * BLOCK, BLOCK), :],
                target.at[:, pl.ds(part * BLOCK, BLOCK), :],
                sems.at[which, part],
            )
            for part in range(ROWS // BLOCK)
        ]

    heat_loads = pieces(heat_hbm, heat_in, in_sem, 0)
    fluid_loads = pieces(fluid_hbm, fluid_in, in_sem, 1)
    heat_stores = pieces(heat_change, heat_out, out_sem, 0)
    fluid_stores = pieces(fluid_change, fluid_out, out_sem, 1)
    for part in range(ROWS // BLOCK):
        fluid_loads[part].start()
        heat_loads[part].start()
    for load in plane_loads:
        load.wait()
    for part in range(ROWS // BLOCK):
        fluid_loads[part].wait()
        heat_loads[part].wait()
        for row in range(part * BLOCK, (part + 1) * BLOCK, 8):
            rows = slice(row, row + 8)
            speed, memory = speed_ref[rows], memory_ref[rows]
            effect_a, effect_b = effect_a_ref[rows], effect_b_ref[rows]
            ratio = memory / effect_a
            argument = 0.5 * speed * jnp.exp(ratio)
            friction = effect_a * jnp.log(argument + jnp.sqrt(argument * argument + 1.0))
            root_term = jnp.sqrt(4.0 * jnp.exp(-2.0 * ratio) + speed * speed)
            effective = clamping_ref[rows] - fluid_in[0, rows]
            traction = effective * friction
            power = HEAT_GAIN * traction * speed
            memory_change = effect_b * (jnp.exp((REF_FRICTION - memory) / effect_b) - speed)
            memory_out[rows] = memory_change
            heat, fluid = heat_in[0, rows], fluid_in[0, rows]
            heat_above, fluid_above = heat_in[1, rows], fluid_in[1, rows]
            heat_below, fluid_below = heat_above, fluid_above
            for point in range(POINTS):
                bent = heat_below - 2.0 * heat
                pressed = fluid_below - 2.0 * fluid
                if point + 1 < POINTS:
                    bent = bent + heat_above
                    pressed = pressed + fluid_above
                warmed = HEAT_DIFFUSIVITY * bent + math.exp(-((point / HEAT_WIDTH) ** 2)) * power
                pressed = FLUID_DIFFUSIVITY * pressed + FLUID_TOGGLE * warmed
                heat_change[point, rows] = warmed
                fluid_change[point, rows] = pressed
                if point == 0:
                    extra = (
                        friction * pressed - effective * (speed / root_term) * memory_change
                    )
                    numerator_out[rows] = extra + RELAXATION * (
                        ambient_ref[rows] - DAMPING * speed - traction
                    )
                    denominator_out[rows] = effective * effect_a / root_term + DAMPING
                heat_below, fluid_below = heat, fluid
                heat, fluid = heat_above, fluid_above
                if point + 2 < POINTS:
                    heat_above, fluid_above = heat_in[point + 2, rows], fluid_in[point + 2, rows]
        heat_stores[part].start()
        fluid_stores[part].start()
    memory_store.start()
    memory_store.wait()
    for part in range(ROWS // BLOCK):
        heat_stores[part].wait()
        fluid_stores[part].wait()


def whole(count):
    return [pl.BlockSpec(memory_space=pltpu.VMEM)] * count


def anywhere(count):
    return [pl.BlockSpec(memory_space=pltpu.HBM)] * count


def in_hbm(*arrays):
    return [pltpu.with_memory_space_constraint(jnp.asarray(x), pltpu.HBM) for x in arrays]


def cost(flops, moved):
    return pl.CostEstimate(flops=flops, bytes_accessed=moved, transcendentals=0)


def shape(*dims):
    return jax.ShapeDtypeStruct(dims, F32)


BLOCK = 16


def grant(mebibytes):
    return pltpu.CompilerParams(vmem_limit_bytes=mebibytes * 1024 * 1024)


def shards(
    sliding_speed,
    offset_displacement,
    contact_memory,
    clamping_traction,
    instant_effect_a,
    healing_effect_b,
    ambient_traction,
    heat_level,
    fluid_load,
):
    depth_forward = depth_table().reshape(PAIRS, PAIR_MODES, DEPTH)
    coarse_forward, coarse_inverse = coarse_tables()
    fine_forward, fine_inverse = fine_tables()
    small = ROWS * COLS * 4
    groups = [
        [(2 * pair + half) * STRIKE_PARTS + part for part, half in PIECES] for pair in range(PAIRS)
    ]

    def over_depth(pieces):
        return lax.all_to_all(pieces, "depth", split_axis=0, concat_axis=0)

    def over_pair(pieces):
        pieces = pieces.reshape(PAIR_SIZE, 1, MODES * LANES)
        moved = lax.all_to_all(
            pieces, ("depth", "strike"), split_axis=0, concat_axis=0, axis_index_groups=groups
        )
        return moved.reshape(PAIR_ROWS, LANES)

    sent, depth_part = pl.pallas_call(
        field_kernel,
        out_shape=(
            shape(DEPTH_PARTS, ROWS, LANES),
            pltpu.VMEM((2 * PAIR_MODES, DEPTH), BF16),
        ),
        in_specs=anywhere(3),
        out_specs=whole(2),
        scratch_shapes=[pltpu.VMEM((ROWS, COLS), F32)] * 2
        + [pltpu.SemaphoreType.DMA((2 + TABLE_CHUNKS,))],
        compiler_params=grant(4),
        cost_estimate=cost(2 * ROWS * COLS, 12 * small),
    )(*in_hbm(sliding_speed, offset_displacement, halves(depth_forward)))
    columns = over_depth(sent)

    modes = pl.pallas_call(
        depth_kernel,
        out_shape=shape(PAIR_ROWS, LANES),
        in_specs=whole(2),
        out_specs=pl.BlockSpec(memory_space=pltpu.VMEM),
        compiler_params=grant(10),
        cost_estimate=cost(6 * PAIR_MODES * DEPTH * LANES, 12 * small),
    )(columns.reshape(DEPTH, LANES), depth_part)

    filtered = pl.pallas_call(
        strike_kernel,
        out_shape=shape(PAIR_ROWS, LANES),
        in_specs=whole(6),
        out_specs=pl.BlockSpec(memory_space=pltpu.VMEM),
        compiler_params=grant(6),
        cost_estimate=cost(6 * 4 * 256 * 256 * LANES, 15 * small),
    )(
        over_pair(modes),
        halves(coarse_forward),
        halves(fine_forward),
        halves(fine_inverse),
        halves(coarse_inverse),
        class_tables(),
    )

    sent = pl.pallas_call(
        depth_back_kernel,
        out_shape=shape(DEPTH, LANES),
        in_specs=whole(2),
        out_specs=pl.BlockSpec(memory_space=pltpu.HBM),
        scratch_shapes=[pltpu.VMEM((DEPTH, LANES), F32), pltpu.SemaphoreType.DMA((BACK_CHUNKS,))],
        compiler_params=grant(10),
        cost_estimate=cost(6 * PAIR_MODES * DEPTH * LANES, 12 * small),
    )(over_pair(filtered), depth_part)
    parts = over_depth(sent.reshape(DEPTH_PARTS, ROWS, LANES))

    memory_change, numerator, denominator, heat_level_change, fluid_load_change = pl.pallas_call(
        stencil_kernel,
        out_shape=(
            shape(ROWS, COLS),
            pltpu.VMEM((ROWS, COLS), F32),
            pltpu.VMEM((ROWS, COLS), F32),
            shape(POINTS, ROWS, COLS),
            shape(POINTS, ROWS, COLS),
        ),
        in_specs=anywhere(8),
        out_specs=anywhere(1) + whole(2) + anywhere(2),
        scratch_shapes=[pltpu.VMEM((ROWS, COLS), F32)] * 7
        + [pltpu.VMEM((POINTS, ROWS, COLS), F32)] * 4
        + [pltpu.SemaphoreType.DMA((2, ROWS // BLOCK))] * 2
        + [pltpu.SemaphoreType.DMA((7,))],
        compiler_params=grant(20),
        cost_estimate=cost(18 * POINTS * ROWS * COLS, 137 * small),
    )(
        *in_hbm(
            sliding_speed,
            contact_memory,
            clamping_traction,
            instant_effect_a,
            healing_effect_b,
            ambient_traction,
            heat_level,
            fluid_load,
        )
    )

    sliding_acceleration = pl.pallas_call(
        final_kernel,
        out_shape=shape(ROWS, COLS),
        in_specs=whole(3),
        out_specs=pl.BlockSpec(memory_space=pltpu.VMEM),
        compiler_params=grant(4),
        cost_estimate=cost(5 * ROWS * COLS, 7 * small),
    )(parts, numerator, denominator)
    return (sliding_acceleration, memory_change, heat_level_change, fluid_load_change)


def solution(mesh):
    plane = P("depth", "strike")
    block = P(None, "depth", "strike")
    return jax.shard_map(
        shards,
        mesh=mesh,
        in_specs=(plane,) * 7 + (block,) * 2,
        out_specs=(plane, plane, block, block),
        check_vma=False,
    )
```

```python
import math

import jax
import jax.numpy as jnp
import ml_dtypes
import numpy as np
from jax import lax
from jax.experimental import pallas as pl
from jax.experimental.pallas import tpu as pltpu
from jax.sharding import PartitionSpec as P

HEAT_GAIN = 0.05
HEAT_DIFFUSIVITY = 0.3
FLUID_DIFFUSIVITY = 0.45
FLUID_TOGGLE = 0.6
REF_FRICTION = 0.5
DAMPING = 0.5
RELAXATION = 0.2
ELASTIC = 4.0 / 3.0
HEAT_WIDTH = 4.0

DEPTH = 768
STRIKE = 8192
ROWS = 96
COLS = 256
POINTS = 32
DEPTH_PARTS = 8
STRIKE_PARTS = 32
LANES = 128
COARSE = STRIKE // LANES
CLASSES = COARSE // 2 + 1
PAIRS = 4
PAIR_MODES = DEPTH // PAIRS
PAIR_SIZE = 2 * STRIKE_PARTS
MODES = 3
PAIR_ROWS = PAIR_SIZE * MODES
TABLE_CHUNKS = 1
BACK_CHUNKS = 6
SPEC_ROWS = 112

ORDER = "hxzc"
Z_FIRST = 5
SIZES = {"h": 2, "x": 2, "z": 8, "c": 2}
WEIGHTS = {name: math.prod(SIZES[k] for k in ORDER[at + 1 :]) for at, name in enumerate(ORDER)}
DIGITS = [
    {name: place // WEIGHTS[name] % SIZES[name] for name in ORDER} for place in range(PAIR_SIZE)
]
PIECES = [(16 * d["x"] + 2 * ((d["z"] + Z_FIRST) % 8) + d["c"], d["h"]) for d in DIGITS]

F32 = jnp.float32
BF16 = jnp.bfloat16


def halves(table):
    high = table.astype(ml_dtypes.bfloat16)
    low = (table - high.astype(np.float64)).astype(ml_dtypes.bfloat16)
    return np.concatenate([high, low], -2)


def depth_table():
    index = np.arange(DEPTH)
    angle = 2.0 * np.pi / DEPTH * (index[:, None] * index[None, :] % DEPTH)
    return np.cos(angle) + np.sin(angle)


def coarse_tables():
    angle = 2.0 * np.pi / COARSE * (np.arange(CLASSES)[:, None] * np.arange(COARSE)[None, :] % COARSE)
    forward = np.zeros((2, SPEC_ROWS, COARSE, MODES))
    inverse = np.zeros((COARSE, MODES, 2, SPEC_ROWS))
    weight = np.where(np.arange(CLASSES) % (COARSE // 2) == 0, 1.0, 2.0)[:, None]
    for mode in range(MODES):
        at = np.arange(CLASSES) * MODES + mode
        forward[0, at, :, mode] = np.cos(angle)
        forward[1, at, :, mode] = -np.sin(angle)
        inverse[:, mode, 0, at] = (weight * np.cos(angle)).T
        inverse[:, mode, 1, at] = (-weight * np.sin(angle)).T
    order = [2 * part + half for part, half in PIECES]
    return (
        forward[:, :, order].reshape(2 * SPEC_ROWS, PAIR_ROWS),
        inverse[order].reshape(PAIR_ROWS, 2 * SPEC_ROWS),
    )


def fine_tables():
    index = np.arange(LANES)
    angle = 2.0 * np.pi / LANES * (index[:, None] * index[None, :] % LANES)
    cosine, sine = np.cos(angle), np.sin(angle)
    forward = np.block([[cosine, -sine], [sine, cosine]])
    inverse = np.block([[cosine, sine], [-sine, cosine]])
    return forward, inverse


def class_tables():
    row = np.arange(SPEC_ROWS)
    k_one = np.minimum(row // MODES, CLASSES - 1)
    lane = np.arange(LANES)
    angle = 2.0 * np.pi / STRIKE * (k_one[:, None] * lane[None, :])
    wave = k_one[:, None] + COARSE * lane[None, :]
    strike_wave = 2.0 * np.pi / STRIKE * np.minimum(wave, STRIKE - wave)
    offset = np.broadcast_to((row % MODES * PAIR_SIZE)[:, None], (SPEC_ROWS, LANES))
    tables = (np.cos(angle), np.sin(angle), strike_wave * strike_wave, offset)
    return np.stack(tables).astype(np.float32)


def split(values):
    high = values.astype(BF16)
    return high, (values - high.astype(F32)).astype(BF16)


def mm(left, right):
    return jnp.dot(left, right, preferred_element_type=F32)


def table_first(table, values):
    rows = table.shape[0] // 2
    v_high, v_low = split(values)
    both = mm(table, v_high)
    return both[:rows] + (both[rows:] + mm(table[:rows], v_low))


def table_last(values, table):
    rows, depth = values.shape
    v_high, v_low = split(values)
    both = mm(jnp.concatenate([v_high, v_low], 0), table[:depth])
    return both[:rows] + (both[rows:] + mm(v_high, table[depth:]))


def table_turned(table, values):
    rows = table.shape[0] // 2
    v_high, v_low = split(values)

    def product(left, right):
        return lax.dot_general(
            left, right, (((0,), (0,)), ((), ())), preferred_element_type=F32
        )

    return product(table[:rows], v_high) + (
        product(table[:rows], v_low) + product(table[rows:], v_high)
    )


def field_kernel(speed_hbm, slip_hbm, table_hbm, out_ref, table_out, speed_ref, slip_ref, sems):
    pair = lax.axis_index("depth") // 2
    loads = [
        pltpu.make_async_copy(source, target, sems.at[at])
        for at, (source, target) in enumerate(((speed_hbm, speed_ref), (slip_hbm, slip_ref)))
    ]
    chunk = 2 * PAIR_MODES // TABLE_CHUNKS
    for part in range(TABLE_CHUNKS):
        rows = pl.ds(part * chunk, chunk)
        loads.append(
            pltpu.make_async_copy(
                table_hbm.at[pair, rows], table_out.at[rows], sems.at[2 + part]
            )
        )
    for load in loads:
        load.start()
    loads[0].wait()
    loads[1].wait()
    field = speed_ref[...] + RELAXATION * slip_ref[...]
    for part in range(DEPTH_PARTS):
        half = part % 2
        out_ref[part] = field[:, half * LANES : (half + 1) * LANES]
    for load in loads[2:]:
        load.wait()


def depth_kernel(fields_ref, table_ref, out_ref):
    modes = table_first(table_ref[...], fields_ref[...])
    for slot in range(MODES):
        out_ref[pl.ds(slot, PAIR_SIZE, stride=MODES), :] = modes[
            slot * PAIR_SIZE : (slot + 1) * PAIR_SIZE
        ]


def strike_kernel(modes_ref, coarse_ref, fine_ref, back_ref, out_table, class_ref, out_ref):
    cosine, sine = class_ref[0], class_ref[1]
    depth_pos, strike_pos = lax.axis_index("depth"), lax.axis_index("strike")
    place = (
        depth_pos % 2 * WEIGHTS["h"]
        + strike_pos // 16 * WEIGHTS["x"]
        + (strike_pos // 2 + 8 - Z_FIRST) % 8 * WEIGHTS["z"]
        + strike_pos % 2 * WEIGHTS["c"]
    )
    base = depth_pos // 2 * PAIR_MODES + place
    depth_index = class_ref[3] + base.astype(F32)
    depth_wave = 2.0 * math.pi / DEPTH * jnp.minimum(depth_index, DEPTH - depth_index)
    depth_square = depth_wave * depth_wave
    strike_square = class_ref[2]
    wave_square = strike_square + depth_square
    kernel = (
        (-0.5 / (DEPTH * STRIKE))
        * (strike_square * ELASTIC + depth_square)
        / jnp.sqrt(jnp.where(wave_square > 0, wave_square, 1.0))
    )
    coarse = table_first(coarse_ref[...], modes_ref[...])
    real, imag = coarse[:SPEC_ROWS], coarse[SPEC_ROWS:]
    turned = jnp.concatenate([real * cosine + imag * sine, imag * cosine - real * sine], 1)
    spectrum = table_last(turned, fine_ref[...])
    spectrum = spectrum * jnp.concatenate([kernel, kernel], 1)
    back = table_last(spectrum, back_ref[...])
    real, imag = back[:, :LANES], back[:, LANES:]
    turned = jnp.concatenate([real * cosine - imag * sine, imag * cosine + real * sine], 0)
    out_ref[...] = table_first(out_table[...], turned)


def depth_back_kernel(modes_ref, table_ref, out_hbm, out_ref, sems):
    modes = jnp.concatenate(
        [modes_ref[pl.ds(slot, PAIR_SIZE, stride=MODES), :] for slot in range(MODES)], 0
    )
    stores = []
    for part in range(BACK_CHUNKS):
        rows = slice(part * DEPTH // BACK_CHUNKS, (part + 1) * DEPTH // BACK_CHUNKS)
        out_ref[rows] = table_turned(table_ref[:, rows], modes)
        stores.append(pltpu.make_async_copy(out_ref.at[rows], out_hbm.at[rows], sems.at[part]))
        stores[-1].start()
    for store in stores:
        store.wait()


def final_kernel(parts_ref, numerator_ref, denominator_ref, out_ref):
    for half in range(2):
        lanes = slice(half * LANES, (half + 1) * LANES)
        filtered = (parts_ref[half] + parts_ref[half + 2]) + (
            parts_ref[half + 4] + parts_ref[half + 6]
        )
        out_ref[:, lanes] = (filtered + numerator_ref[:, lanes]) / denominator_ref[:, lanes]


def stencil_kernel(
    speed_hbm,
    memory_hbm,
    clamping_hbm,
    effect_a_hbm,
    effect_b_hbm,
    ambient_hbm,
    heat_hbm,
    fluid_hbm,
    memory_hbm_out,
    numerator_out,
    denominator_out,
    heat_out,
    fluid_out,
    speed_ref,
    memory_ref,
    clamping_ref,
    effect_a_ref,
    effect_b_ref,
    ambient_ref,
    memory_out,
    heat_in,
    fluid_in,
    heat_change,
    fluid_change,
    in_sem,
    out_sem,
    plane_sem,
):
    plane_loads = [
        pltpu.make_async_copy(source, target, plane_sem.at[at])
        for at, (source, target) in enumerate(
            (
                (speed_hbm, speed_ref),
                (memory_hbm, memory_ref),
                (clamping_hbm, clamping_ref),
                (effect_a_hbm, effect_a_ref),
                (effect_b_hbm, effect_b_ref),
                (ambient_hbm, ambient_ref),
            )
        )
    ]
    memory_store = pltpu.make_async_copy(memory_out, memory_hbm_out, plane_sem.at[6])
    for load in plane_loads:
        load.start()

    def pieces(source, target, sems, which):
        return [
            pltpu.make_async_copy(
                source.at[:, pl.ds(part * BLOCK, BLOCK), :],
                target.at[:, pl.ds(part * BLOCK, BLOCK), :],
                sems.at[which, part],
            )
            for part in range(ROWS // BLOCK)
        ]

    heat_loads = pieces(heat_hbm, heat_in, in_sem, 0)
    fluid_loads = pieces(fluid_hbm, fluid_in, in_sem, 1)
    heat_stores = pieces(heat_change, heat_out, out_sem, 0)
    fluid_stores = pieces(fluid_change, fluid_out, out_sem, 1)
    for part in range(ROWS // BLOCK):
        fluid_loads[part].start()
        heat_loads[part].start()
    for load in plane_loads:
        load.wait()
    for part in range(ROWS // BLOCK):
        fluid_loads[part].wait()
        heat_loads[part].wait()
        for row in range(part * BLOCK, (part + 1) * BLOCK, 8):
            rows = slice(row, row + 8)
            speed, memory = speed_ref[rows], memory_ref[rows]
            effect_a, effect_b = effect_a_ref[rows], effect_b_ref[rows]
            ratio = memory / effect_a
            argument = 0.5 * speed * jnp.exp(ratio)
            friction = effect_a * jnp.log(argument + jnp.sqrt(argument * argument + 1.0))
            root_term = jnp.sqrt(4.0 * jnp.exp(-2.0 * ratio) + speed * speed)
            effective = clamping_ref[rows] - fluid_in[0, rows]
            traction = effective * friction
            power = HEAT_GAIN * traction * speed
            memory_change = effect_b * (jnp.exp((REF_FRICTION - memory) / effect_b) - speed)
            memory_out[rows] = memory_change
            heat, fluid = heat_in[0, rows], fluid_in[0, rows]
            heat_above, fluid_above = heat_in[1, rows], fluid_in[1, rows]
            heat_below, fluid_below = heat_above, fluid_above
            for point in range(POINTS):
                bent = heat_below - 2.0 * heat
                pressed = fluid_below - 2.0 * fluid
                if point + 1 < POINTS:
                    bent = bent + heat_above
                    pressed = pressed + fluid_above
                warmed = HEAT_DIFFUSIVITY * bent + math.exp(-((point / HEAT_WIDTH) ** 2)) * power
                pressed = FLUID_DIFFUSIVITY * pressed + FLUID_TOGGLE * warmed
                heat_change[point, rows] = warmed
                fluid_change[point, rows] = pressed
                if point == 0:
                    extra = (
                        friction * pressed - effective * (speed / root_term) * memory_change
                    )
                    numerator_out[rows] = extra + RELAXATION * (
                        ambient_ref[rows] - DAMPING * speed - traction
                    )
                    denominator_out[rows] = effective * effect_a / root_term + DAMPING
                heat_below, fluid_below = heat, fluid
                heat, fluid = heat_above, fluid_above
                if point + 2 < POINTS:
                    heat_above, fluid_above = heat_in[point + 2, rows], fluid_in[point + 2, rows]
        heat_stores[part].start()
        fluid_stores[part].start()
    memory_store.start()
    memory_store.wait()
    for part in range(ROWS // BLOCK):
        heat_stores[part].wait()
        fluid_stores[part].wait()


def whole(count):
    return [pl.BlockSpec(memory_space=pltpu.VMEM)] * count


def anywhere(count):
    return [pl.BlockSpec(memory_space=pltpu.HBM)] * count


def in_hbm(*arrays):
    return [pltpu.with_memory_space_constraint(jnp.asarray(x), pltpu.HBM) for x in arrays]


def cost(flops, moved):
    return pl.CostEstimate(flops=flops, bytes_accessed=moved, transcendentals=0)


def shape(*dims):
    return jax.ShapeDtypeStruct(dims, F32)


BLOCK = 16


def grant(mebibytes):
    return pltpu.CompilerParams(vmem_limit_bytes=mebibytes * 1024 * 1024)


def shards(
    sliding_speed,
    offset_displacement,
    contact_memory,
    clamping_traction,
    instant_effect_a,
    healing_effect_b,
    ambient_traction,
    heat_level,
    fluid_load,
):
    depth_forward = depth_table().reshape(PAIRS, PAIR_MODES, DEPTH)
    coarse_forward, coarse_inverse = coarse_tables()
    fine_forward, fine_inverse = fine_tables()
    small = ROWS * COLS * 4
    groups = [
        [(2 * pair + half) * STRIKE_PARTS + part for part, half in PIECES] for pair in range(PAIRS)
    ]

    def over_depth(pieces):
        return lax.all_to_all(pieces, "depth", split_axis=0, concat_axis=0)

    def over_pair(pieces):
        pieces = pieces.reshape(PAIR_SIZE, 1, MODES * LANES)
        moved = lax.all_to_all(
            pieces, ("depth", "strike"), split_axis=0, concat_axis=0, axis_index_groups=groups
        )
        return moved.reshape(PAIR_ROWS, LANES)

    sent, depth_part = pl.pallas_call(
        field_kernel,
        out_shape=(
            shape(DEPTH_PARTS, ROWS, LANES),
            pltpu.VMEM((2 * PAIR_MODES, DEPTH), BF16),
        ),
        in_specs=anywhere(3),
        out_specs=whole(2),
        scratch_shapes=[pltpu.VMEM((ROWS, COLS), F32)] * 2
        + [pltpu.SemaphoreType.DMA((2 + TABLE_CHUNKS,))],
        compiler_params=grant(4),
        cost_estimate=cost(2 * ROWS * COLS, 12 * small),
    )(*in_hbm(sliding_speed, offset_displacement, halves(depth_forward)))
    columns = over_depth(sent)

    modes = pl.pallas_call(
        depth_kernel,
        out_shape=shape(PAIR_ROWS, LANES),
        in_specs=whole(2),
        out_specs=pl.BlockSpec(memory_space=pltpu.VMEM),
        compiler_params=grant(10),
        cost_estimate=cost(6 * PAIR_MODES * DEPTH * LANES, 12 * small),
    )(columns.reshape(DEPTH, LANES), depth_part)

    filtered = pl.pallas_call(
        strike_kernel,
        out_shape=shape(PAIR_ROWS, LANES),
        in_specs=whole(6),
        out_specs=pl.BlockSpec(memory_space=pltpu.VMEM),
        compiler_params=grant(6),
        cost_estimate=cost(6 * 4 * 256 * 256 * LANES, 15 * small),
    )(
        over_pair(modes),
        halves(coarse_forward),
        halves(fine_forward),
        halves(fine_inverse),
        halves(coarse_inverse),
        class_tables(),
    )

    sent = pl.pallas_call(
        depth_back_kernel,
        out_shape=shape(DEPTH, LANES),
        in_specs=whole(2),
        out_specs=pl.BlockSpec(memory_space=pltpu.HBM),
        scratch_shapes=[pltpu.VMEM((DEPTH, LANES), F32), pltpu.SemaphoreType.DMA((BACK_CHUNKS,))],
        compiler_params=grant(10),
        cost_estimate=cost(6 * PAIR_MODES * DEPTH * LANES, 12 * small),
    )(over_pair(filtered), depth_part)
    parts = over_depth(sent.reshape(DEPTH_PARTS, ROWS, LANES))

    memory_change, numerator, denominator, heat_level_change, fluid_load_change = pl.pallas_call(
        stencil_kernel,
        out_shape=(
            shape(ROWS, COLS),
            pltpu.VMEM((ROWS, COLS), F32),
            pltpu.VMEM((ROWS, COLS), F32),
            shape(POINTS, ROWS, COLS),
            shape(POINTS, ROWS, COLS),
        ),
        in_specs=anywhere(8),
        out_specs=anywhere(1) + whole(2) + anywhere(2),
        scratch_shapes=[pltpu.VMEM((ROWS, COLS), F32)] * 7
        + [pltpu.VMEM((POINTS, ROWS, COLS), F32)] * 4
        + [pltpu.SemaphoreType.DMA((2, ROWS // BLOCK))] * 2
        + [pltpu.SemaphoreType.DMA((7,))],
        compiler_params=grant(20),
        cost_estimate=cost(18 * POINTS * ROWS * COLS, 137 * small),
    )(
        *in_hbm(
            sliding_speed,
            contact_memory,
            clamping_traction,
            instant_effect_a,
            healing_effect_b,
            ambient_traction,
            heat_level,
            fluid_load,
        )
    )

    sliding_acceleration = pl.pallas_call(
        final_kernel,
        out_shape=shape(ROWS, COLS),
        in_specs=whole(3),
        out_specs=pl.BlockSpec(memory_space=pltpu.VMEM),
        compiler_params=grant(4),
        cost_estimate=cost(5 * ROWS * COLS, 7 * small),
    )(parts, numerator, denominator)
    return (sliding_acceleration, memory_change, heat_level_change, fluid_load_change)


def solution(mesh):
    plane = P("depth", "strike")
    block = P(None, "depth", "strike")
    return jax.shard_map(
        shards,
        mesh=mesh,
        in_specs=(plane,) * 7 + (block,) * 2,
        out_specs=(plane, plane, block, block),
        check_vma=False,
    )
```

```python
import math

import jax
import jax.numpy as jnp
import ml_dtypes
import numpy as np
from jax import lax
from jax.experimental import pallas as pl
from jax.experimental.pallas import tpu as pltpu
from jax.sharding import PartitionSpec as P

HEAT_GAIN = 0.05
HEAT_DIFFUSIVITY = 0.3
FLUID_DIFFUSIVITY = 0.45
FLUID_TOGGLE = 0.6
REF_FRICTION = 0.5
DAMPING = 0.5
RELAXATION = 0.2
ELASTIC = 4.0 / 3.0
HEAT_WIDTH = 4.0

DEPTH = 768
STRIKE = 8192
ROWS = 96
COLS = 256
POINTS = 32
DEPTH_PARTS = 8
STRIKE_PARTS = 32
LANES = 128
COARSE = STRIKE // LANES
CLASSES = COARSE // 2 + 1
PAIRS = 4
PAIR_MODES = DEPTH // PAIRS
PAIR_SIZE = 2 * STRIKE_PARTS
MODES = 3
PAIR_ROWS = PAIR_SIZE * MODES
TABLE_CHUNKS = 1
BACK_CHUNKS = 6
SPEC_ROWS = 112

ORDER = "hxzc"
Z_FIRST = 5
DEPTH_ORDER = [7, 4, 5, 6, 3, 0, 1, 2]
SIZES = {"h": 2, "x": 2, "z": 8, "c": 2}
WEIGHTS = {name: math.prod(SIZES[k] for k in ORDER[at + 1 :]) for at, name in enumerate(ORDER)}
DIGITS = [
    {name: place // WEIGHTS[name] % SIZES[name] for name in ORDER} for place in range(PAIR_SIZE)
]
PIECES = [(16 * d["x"] + 2 * ((d["z"] + Z_FIRST) % 8) + d["c"], d["h"]) for d in DIGITS]

F32 = jnp.float32
BF16 = jnp.bfloat16


def halves(table):
    high = table.astype(ml_dtypes.bfloat16)
    low = (table - high.astype(np.float64)).astype(ml_dtypes.bfloat16)
    return np.concatenate([high, low], -2)


def depth_table():
    index = np.arange(DEPTH)
    angle = 2.0 * np.pi / DEPTH * (index[:, None] * index[None, :] % DEPTH)
    table = (np.cos(angle) + np.sin(angle)).reshape(DEPTH, DEPTH_PARTS, ROWS)
    return table[:, DEPTH_ORDER].reshape(DEPTH, DEPTH)


def coarse_tables():
    angle = 2.0 * np.pi / COARSE * (np.arange(CLASSES)[:, None] * np.arange(COARSE)[None, :] % COARSE)
    forward = np.zeros((2, SPEC_ROWS, COARSE, MODES))
    inverse = np.zeros((COARSE, MODES, 2, SPEC_ROWS))
    weight = np.where(np.arange(CLASSES) % (COARSE // 2) == 0, 1.0, 2.0)[:, None]
    for mode in range(MODES):
        at = np.arange(CLASSES) * MODES + mode
        forward[0, at, :, mode] = np.cos(angle)
        forward[1, at, :, mode] = -np.sin(angle)
        inverse[:, mode, 0, at] = (weight * np.cos(angle)).T
        inverse[:, mode, 1, at] = (-weight * np.sin(angle)).T
    order = [2 * part + half for part, half in PIECES]
    return (
        forward[:, :, order].reshape(2 * SPEC_ROWS, PAIR_ROWS),
        inverse[order].reshape(PAIR_ROWS, 2 * SPEC_ROWS),
    )


def fine_tables():
    index = np.arange(LANES)
    angle = 2.0 * np.pi / LANES * (index[:, None] * index[None, :] % LANES)
    cosine, sine = np.cos(angle), np.sin(angle)
    forward = np.block([[cosine, -sine], [sine, cosine]])
    inverse = np.block([[cosine, sine], [-sine, cosine]])
    return forward, inverse


def class_tables():
    row = np.arange(SPEC_ROWS)
    k_one = np.minimum(row // MODES, CLASSES - 1)
    lane = np.arange(LANES)
    angle = 2.0 * np.pi / STRIKE * (k_one[:, None] * lane[None, :])
    wave = k_one[:, None] + COARSE * lane[None, :]
    strike_wave = 2.0 * np.pi / STRIKE * np.minimum(wave, STRIKE - wave)
    offset = np.broadcast_to((row % MODES * PAIR_SIZE)[:, None], (SPEC_ROWS, LANES))
    tables = (np.cos(angle), np.sin(angle), strike_wave * strike_wave, offset)
    return np.stack(tables).astype(np.float32)


def split(values):
    high = values.astype(BF16)
    return high, (values - high.astype(F32)).astype(BF16)


def mm(left, right):
    return jnp.dot(left, right, preferred_element_type=F32)


def table_first(table, values):
    rows = table.shape[0] // 2
    v_high, v_low = split(values)
    both = mm(table, v_high)
    return both[:rows] + (both[rows:] + mm(table[:rows], v_low))


def table_last(values, table):
    rows, depth = values.shape
    v_high, v_low = split(values)
    both = mm(jnp.concatenate([v_high, v_low], 0), table[:depth])
    return both[:rows] + (both[rows:] + mm(v_high, table[depth:]))


def table_turned(table, values):
    rows = table.shape[0] // 2
    v_high, v_low = split(values)

    def product(left, right):
        return lax.dot_general(
            left, right, (((0,), (0,)), ((), ())), preferred_element_type=F32
        )

    return product(table[:rows], v_high) + (
        product(table[:rows], v_low) + product(table[rows:], v_high)
    )


def field_kernel(speed_hbm, slip_hbm, table_hbm, out_ref, table_out, speed_ref, slip_ref, sems):
    pair = lax.axis_index("depth") // 2
    loads = [
        pltpu.make_async_copy(source, target, sems.at[at])
        for at, (source, target) in enumerate(((speed_hbm, speed_ref), (slip_hbm, slip_ref)))
    ]
    chunk = 2 * PAIR_MODES // TABLE_CHUNKS
    for part in range(TABLE_CHUNKS):
        rows = pl.ds(part * chunk, chunk)
        loads.append(
            pltpu.make_async_copy(
                table_hbm.at[pair, rows], table_out.at[rows], sems.at[2 + part]
            )
        )
    for load in loads:
        load.start()
    loads[0].wait()
    loads[1].wait()
    field = speed_ref[...] + RELAXATION * slip_ref[...]
    for part in range(DEPTH_PARTS):
        half = DEPTH_ORDER[part] % 2
        out_ref[part] = field[:, half * LANES : (half + 1) * LANES]
    for load in loads[2:]:
        load.wait()


def depth_kernel(fields_ref, table_ref, out_ref):
    modes = table_first(table_ref[...], fields_ref[...])
    for slot in range(MODES):
        out_ref[pl.ds(slot, PAIR_SIZE, stride=MODES), :] = modes[
            slot * PAIR_SIZE : (slot + 1) * PAIR_SIZE
        ]


def strike_kernel(modes_ref, coarse_ref, fine_ref, back_ref, out_table, class_ref, out_ref):
    cosine, sine = class_ref[0], class_ref[1]
    depth_pos, strike_pos = lax.axis_index("depth"), lax.axis_index("strike")
    place = (
        depth_pos % 2 * WEIGHTS["h"]
        + strike_pos // 16 * WEIGHTS["x"]
        + (strike_pos // 2 + 8 - Z_FIRST) % 8 * WEIGHTS["z"]
        + strike_pos % 2 * WEIGHTS["c"]
    )
    base = depth_pos // 2 * PAIR_MODES + place
    depth_index = class_ref[3] + base.astype(F32)
    depth_wave = 2.0 * math.pi / DEPTH * jnp.minimum(depth_index, DEPTH - depth_index)
    depth_square = depth_wave * depth_wave
    strike_square = class_ref[2]
    wave_square = strike_square + depth_square
    kernel = (
        (-0.5 / (DEPTH * STRIKE))
        * (strike_square * ELASTIC + depth_square)
        / jnp.sqrt(jnp.where(wave_square > 0, wave_square, 1.0))
    )
    coarse = table_first(coarse_ref[...], modes_ref[...])
    real, imag = coarse[:SPEC_ROWS], coarse[SPEC_ROWS:]
    turned = jnp.concatenate([real * cosine + imag * sine, imag * cosine - real * sine], 1)
    spectrum = table_last(turned, fine_ref[...])
    spectrum = spectrum * jnp.concatenate([kernel, kernel], 1)
    back = table_last(spectrum, back_ref[...])
    real, imag = back[:, :LANES], back[:, LANES:]
    turned = jnp.concatenate([real * cosine - imag * sine, imag * cosine + real * sine], 0)
    out_ref[...] = table_first(out_table[...], turned)


def depth_back_kernel(modes_ref, table_ref, out_hbm, out_ref, sems):
    modes = jnp.concatenate(
        [modes_ref[pl.ds(slot, PAIR_SIZE, stride=MODES), :] for slot in range(MODES)], 0
    )
    stores = []
    for part in range(BACK_CHUNKS):
        rows = slice(part * DEPTH // BACK_CHUNKS, (part + 1) * DEPTH // BACK_CHUNKS)
        out_ref[rows] = table_turned(table_ref[:, rows], modes)
        stores.append(pltpu.make_async_copy(out_ref.at[rows], out_hbm.at[rows], sems.at[part]))
        stores[-1].start()
    for store in stores:
        store.wait()


def final_kernel(parts_ref, numerator_ref, denominator_ref, out_ref):
    for half in range(2):
        lanes = slice(half * LANES, (half + 1) * LANES)
        one, two, three, four = (
            parts_ref[part] for part in range(DEPTH_PARTS) if DEPTH_ORDER[part] % 2 == half
        )
        filtered = (one + two) + (three + four)
        out_ref[:, lanes] = (filtered + numerator_ref[:, lanes]) / denominator_ref[:, lanes]


def stencil_kernel(
    speed_hbm,
    memory_hbm,
    clamping_hbm,
    effect_a_hbm,
    effect_b_hbm,
    ambient_hbm,
    heat_hbm,
    fluid_hbm,
    memory_hbm_out,
    numerator_out,
    denominator_out,
    heat_out,
    fluid_out,
    speed_ref,
    memory_ref,
    clamping_ref,
    effect_a_ref,
    effect_b_ref,
    ambient_ref,
    memory_out,
    heat_in,
    fluid_in,
    heat_change,
    fluid_change,
    in_sem,
    out_sem,
    plane_sem,
):
    plane_loads = [
        pltpu.make_async_copy(source, target, plane_sem.at[at])
        for at, (source, target) in enumerate(
            (
                (speed_hbm, speed_ref),
                (memory_hbm, memory_ref),
                (clamping_hbm, clamping_ref),
                (effect_a_hbm, effect_a_ref),
                (effect_b_hbm, effect_b_ref),
                (ambient_hbm, ambient_ref),
            )
        )
    ]
    memory_store = pltpu.make_async_copy(memory_out, memory_hbm_out, plane_sem.at[6])
    for load in plane_loads:
        load.start()

    def pieces(source, target, sems, which):
        return [
            pltpu.make_async_copy(
                source.at[:, pl.ds(part * BLOCK, BLOCK), :],
                target.at[:, pl.ds(part * BLOCK, BLOCK), :],
                sems.at[which, part],
            )
            for part in range(ROWS // BLOCK)
        ]

    heat_loads = pieces(heat_hbm, heat_in, in_sem, 0)
    fluid_loads = pieces(fluid_hbm, fluid_in, in_sem, 1)
    heat_stores = pieces(heat_change, heat_out, out_sem, 0)
    fluid_stores = pieces(fluid_change, fluid_out, out_sem, 1)
    for part in range(ROWS // BLOCK):
        fluid_loads[part].start()
        heat_loads[part].start()
    for load in plane_loads:
        load.wait()
    for part in range(ROWS // BLOCK):
        fluid_loads[part].wait()
        heat_loads[part].wait()
        for row in range(part * BLOCK, (part + 1) * BLOCK, 8):
            rows = slice(row, row + 8)
            speed, memory = speed_ref[rows], memory_ref[rows]
            effect_a, effect_b = effect_a_ref[rows], effect_b_ref[rows]
            ratio = memory / effect_a
            argument = 0.5 * speed * jnp.exp(ratio)
            friction = effect_a * jnp.log(argument + jnp.sqrt(argument * argument + 1.0))
            root_term = jnp.sqrt(4.0 * jnp.exp(-2.0 * ratio) + speed * speed)
            effective = clamping_ref[rows] - fluid_in[0, rows]
            traction = effective * friction
            power = HEAT_GAIN * traction * speed
            memory_change = effect_b * (jnp.exp((REF_FRICTION - memory) / effect_b) - speed)
            memory_out[rows] = memory_change
            heat, fluid = heat_in[0, rows], fluid_in[0, rows]
            heat_above, fluid_above = heat_in[1, rows], fluid_in[1, rows]
            heat_below, fluid_below = heat_above, fluid_above
            for point in range(POINTS):
                bent = heat_below - 2.0 * heat
                pressed = fluid_below - 2.0 * fluid
                if point + 1 < POINTS:
                    bent = bent + heat_above
                    pressed = pressed + fluid_above
                warmed = HEAT_DIFFUSIVITY * bent + math.exp(-((point / HEAT_WIDTH) ** 2)) * power
                pressed = FLUID_DIFFUSIVITY * pressed + FLUID_TOGGLE * warmed
                heat_change[point, rows] = warmed
                fluid_change[point, rows] = pressed
                if point == 0:
                    extra = (
                        friction * pressed - effective * (speed / root_term) * memory_change
                    )
                    numerator_out[rows] = extra + RELAXATION * (
                        ambient_ref[rows] - DAMPING * speed - traction
                    )
                    denominator_out[rows] = effective * effect_a / root_term + DAMPING
                heat_below, fluid_below = heat, fluid
                heat, fluid = heat_above, fluid_above
                if point + 2 < POINTS:
                    heat_above, fluid_above = heat_in[point + 2, rows], fluid_in[point + 2, rows]
        heat_stores[part].start()
        fluid_stores[part].start()
    memory_store.start()
    memory_store.wait()
    for part in range(ROWS // BLOCK):
        heat_stores[part].wait()
        fluid_stores[part].wait()


def whole(count):
    return [pl.BlockSpec(memory_space=pltpu.VMEM)] * count


def anywhere(count):
    return [pl.BlockSpec(memory_space=pltpu.HBM)] * count


def in_hbm(*arrays):
    return [pltpu.with_memory_space_constraint(jnp.asarray(x), pltpu.HBM) for x in arrays]


def cost(flops, moved):
    return pl.CostEstimate(flops=flops, bytes_accessed=moved, transcendentals=0)


def shape(*dims):
    return jax.ShapeDtypeStruct(dims, F32)


BLOCK = 16


def grant(mebibytes):
    return pltpu.CompilerParams(vmem_limit_bytes=mebibytes * 1024 * 1024)


def shards(
    sliding_speed,
    offset_displacement,
    contact_memory,
    clamping_traction,
    instant_effect_a,
    healing_effect_b,
    ambient_traction,
    heat_level,
    fluid_load,
):
    depth_forward = depth_table().reshape(PAIRS, PAIR_MODES, DEPTH)
    coarse_forward, coarse_inverse = coarse_tables()
    fine_forward, fine_inverse = fine_tables()
    small = ROWS * COLS * 4
    groups = [
        [(2 * pair + half) * STRIKE_PARTS + part for part, half in PIECES] for pair in range(PAIRS)
    ]

    def over_depth(pieces):
        return lax.all_to_all(
            pieces, "depth", split_axis=0, concat_axis=0, axis_index_groups=[DEPTH_ORDER]
        )

    def over_pair(pieces):
        pieces = pieces.reshape(PAIR_SIZE, 1, MODES * LANES)
        moved = lax.all_to_all(
            pieces, ("depth", "strike"), split_axis=0, concat_axis=0, axis_index_groups=groups
        )
        return moved.reshape(PAIR_ROWS, LANES)

    sent, depth_part = pl.pallas_call(
        field_kernel,
        out_shape=(
            shape(DEPTH_PARTS, ROWS, LANES),
            pltpu.VMEM((2 * PAIR_MODES, DEPTH), BF16),
        ),
        in_specs=anywhere(3),
        out_specs=whole(2),
        scratch_shapes=[pltpu.VMEM((ROWS, COLS), F32)] * 2
        + [pltpu.SemaphoreType.DMA((2 + TABLE_CHUNKS,))],
        compiler_params=grant(4),
        cost_estimate=cost(2 * ROWS * COLS, 12 * small),
    )(*in_hbm(sliding_speed, offset_displacement, halves(depth_forward)))
    columns = over_depth(sent)

    modes = pl.pallas_call(
        depth_kernel,
        out_shape=shape(PAIR_ROWS, LANES),
        in_specs=whole(2),
        out_specs=pl.BlockSpec(memory_space=pltpu.VMEM),
        compiler_params=grant(10),
        cost_estimate=cost(6 * PAIR_MODES * DEPTH * LANES, 12 * small),
    )(columns.reshape(DEPTH, LANES), depth_part)

    filtered = pl.pallas_call(
        strike_kernel,
        out_shape=shape(PAIR_ROWS, LANES),
        in_specs=whole(6),
        out_specs=pl.BlockSpec(memory_space=pltpu.VMEM),
        compiler_params=grant(6),
        cost_estimate=cost(6 * 4 * 256 * 256 * LANES, 15 * small),
    )(
        over_pair(modes),
        halves(coarse_forward),
        halves(fine_forward),
        halves(fine_inverse),
        halves(coarse_inverse),
        class_tables(),
    )

    sent = pl.pallas_call(
        depth_back_kernel,
        out_shape=shape(DEPTH, LANES),
        in_specs=whole(2),
        out_specs=pl.BlockSpec(memory_space=pltpu.HBM),
        scratch_shapes=[pltpu.VMEM((DEPTH, LANES), F32), pltpu.SemaphoreType.DMA((BACK_CHUNKS,))],
        compiler_params=grant(10),
        cost_estimate=cost(6 * PAIR_MODES * DEPTH * LANES, 12 * small),
    )(over_pair(filtered), depth_part)
    parts = over_depth(sent.reshape(DEPTH_PARTS, ROWS, LANES))

    memory_change, numerator, denominator, heat_level_change, fluid_load_change = pl.pallas_call(
        stencil_kernel,
        out_shape=(
            shape(ROWS, COLS),
            pltpu.VMEM((ROWS, COLS), F32),
            pltpu.VMEM((ROWS, COLS), F32),
            shape(POINTS, ROWS, COLS),
            shape(POINTS, ROWS, COLS),
        ),
        in_specs=anywhere(8),
        out_specs=anywhere(1) + whole(2) + anywhere(2),
        scratch_shapes=[pltpu.VMEM((ROWS, COLS), F32)] * 7
        + [pltpu.VMEM((POINTS, ROWS, COLS), F32)] * 4
        + [pltpu.SemaphoreType.DMA((2, ROWS // BLOCK))] * 2
        + [pltpu.SemaphoreType.DMA((7,))],
        compiler_params=grant(20),
        cost_estimate=cost(18 * POINTS * ROWS * COLS, 137 * small),
    )(
        *in_hbm(
            sliding_speed,
            contact_memory,
            clamping_traction,
            instant_effect_a,
            healing_effect_b,
            ambient_traction,
            heat_level,
            fluid_load,
        )
    )

    sliding_acceleration = pl.pallas_call(
        final_kernel,
        out_shape=shape(ROWS, COLS),
        in_specs=whole(3),
        out_specs=pl.BlockSpec(memory_space=pltpu.VMEM),
        compiler_params=grant(4),
        cost_estimate=cost(5 * ROWS * COLS, 7 * small),
    )(parts, numerator, denominator)
    return (sliding_acceleration, memory_change, heat_level_change, fluid_load_change)


def solution(mesh):
    plane = P("depth", "strike")
    block = P(None, "depth", "strike")
    return jax.shard_map(
        shards,
        mesh=mesh,
        in_specs=(plane,) * 7 + (block,) * 2,
        out_specs=(plane, plane, block, block),
        check_vma=False,
    )
```

```python
import math

import jax
import jax.numpy as jnp
import ml_dtypes
import numpy as np
from jax import lax
from jax.experimental import pallas as pl
from jax.experimental.pallas import tpu as pltpu
from jax.sharding import PartitionSpec as P

HEAT_GAIN = 0.05
HEAT_DIFFUSIVITY = 0.3
FLUID_DIFFUSIVITY = 0.45
FLUID_TOGGLE = 0.6
REF_FRICTION = 0.5
DAMPING = 0.5
RELAXATION = 0.2
ELASTIC = 4.0 / 3.0
HEAT_WIDTH = 4.0

DEPTH = 768
STRIKE = 8192
ROWS = 96
COLS = 256
POINTS = 32
DEPTH_PARTS = 8
STRIKE_PARTS = 32
LANES = 128
COARSE = STRIKE // LANES
CLASSES = COARSE // 2 + 1
PAIRS = 4
PAIR_MODES = DEPTH // PAIRS
PAIR_SIZE = 2 * STRIKE_PARTS
MODES = 3
PAIR_ROWS = PAIR_SIZE * MODES
TABLE_CHUNKS = 1
BACK_CHUNKS = 6
SPEC_ROWS = 112

ORDER = "hxzc"
Z_FIRST = 5
DEPTH_ORDER = [3, 0, 1, 2, 7, 4, 5, 6]
SIZES = {"h": 2, "x": 2, "z": 8, "c": 2}
WEIGHTS = {name: math.prod(SIZES[k] for k in ORDER[at + 1 :]) for at, name in enumerate(ORDER)}
DIGITS = [
    {name: place // WEIGHTS[name] % SIZES[name] for name in ORDER} for place in range(PAIR_SIZE)
]
PIECES = [(16 * d["x"] + 2 * ((d["z"] + Z_FIRST) % 8) + d["c"], d["h"]) for d in DIGITS]

F32 = jnp.float32
BF16 = jnp.bfloat16


def halves(table):
    high = table.astype(ml_dtypes.bfloat16)
    low = (table - high.astype(np.float64)).astype(ml_dtypes.bfloat16)
    return np.concatenate([high, low], -2)


def depth_table():
    index = np.arange(DEPTH)
    angle = 2.0 * np.pi / DEPTH * (index[:, None] * index[None, :] % DEPTH)
    table = (np.cos(angle) + np.sin(angle)).reshape(DEPTH, DEPTH_PARTS, ROWS)
    return table[:, DEPTH_ORDER].reshape(DEPTH, DEPTH)


def coarse_tables():
    angle = 2.0 * np.pi / COARSE * (np.arange(CLASSES)[:, None] * np.arange(COARSE)[None, :] % COARSE)
    forward = np.zeros((2, SPEC_ROWS, COARSE, MODES))
    inverse = np.zeros((COARSE, MODES, 2, SPEC_ROWS))
    weight = np.where(np.arange(CLASSES) % (COARSE // 2) == 0, 1.0, 2.0)[:, None]
    for mode in range(MODES):
        at = np.arange(CLASSES) * MODES + mode
        forward[0, at, :, mode] = np.cos(angle)
        forward[1, at, :, mode] = -np.sin(angle)
        inverse[:, mode, 0, at] = (weight * np.cos(angle)).T
        inverse[:, mode, 1, at] = (-weight * np.sin(angle)).T
    order = [2 * part + half for part, half in PIECES]
    return (
        forward[:, :, order].reshape(2 * SPEC_ROWS, PAIR_ROWS),
        inverse[order].reshape(PAIR_ROWS, 2 * SPEC_ROWS),
    )


def fine_tables():
    index = np.arange(LANES)
    angle = 2.0 * np.pi / LANES * (index[:, None] * index[None, :] % LANES)
    cosine, sine = np.cos(angle), np.sin(angle)
    forward = np.block([[cosine, -sine], [sine, cosine]])
    inverse = np.block([[cosine, sine], [-sine, cosine]])
    return forward, inverse


def class_tables():
    row = np.arange(SPEC_ROWS)
    k_one = np.minimum(row // MODES, CLASSES - 1)
    lane = np.arange(LANES)
    angle = 2.0 * np.pi / STRIKE * (k_one[:, None] * lane[None, :])
    wave = k_one[:, None] + COARSE * lane[None, :]
    strike_wave = 2.0 * np.pi / STRIKE * np.minimum(wave, STRIKE - wave)
    offset = np.broadcast_to((row % MODES * PAIR_SIZE)[:, None], (SPEC_ROWS, LANES))
    tables = (np.cos(angle), np.sin(angle), strike_wave * strike_wave, offset)
    return np.stack(tables).astype(np.float32)


def split(values):
    high = values.astype(BF16)
    return high, (values - high.astype(F32)).astype(BF16)


def mm(left, right):
    return jnp.dot(left, right, preferred_element_type=F32)


def table_first(table, values):
    rows = table.shape[0] // 2
    v_high, v_low = split(values)
    both = mm(table, v_high)
    return both[:rows] + (both[rows:] + mm(table[:rows], v_low))


def table_last(values, table):
    rows, depth = values.shape
    v_high, v_low = split(values)
    both = mm(jnp.concatenate([v_high, v_low], 0), table[:depth])
    return both[:rows] + (both[rows:] + mm(v_high, table[depth:]))


def table_turned(table, values):
    rows = table.shape[0] // 2
    v_high, v_low = split(values)

    def product(left, right):
        return lax.dot_general(
            left, right, (((0,), (0,)), ((), ())), preferred_element_type=F32
        )

    return product(table[:rows], v_high) + (
        product(table[:rows], v_low) + product(table[rows:], v_high)
    )


def field_kernel(speed_hbm, slip_hbm, table_hbm, out_ref, table_out, speed_ref, slip_ref, sems):
    pair = lax.axis_index("depth") // 2
    loads = [
        pltpu.make_async_copy(source, target, sems.at[at])
        for at, (source, target) in enumerate(((speed_hbm, speed_ref), (slip_hbm, slip_ref)))
    ]
    chunk = 2 * PAIR_MODES // TABLE_CHUNKS
    for part in range(TABLE_CHUNKS):
        rows = pl.ds(part * chunk, chunk)
        loads.append(
            pltpu.make_async_copy(
                table_hbm.at[pair, rows], table_out.at[rows], sems.at[2 + part]
            )
        )
    for load in loads:
        load.start()
    loads[0].wait()
    loads[1].wait()
    field = speed_ref[...] + RELAXATION * slip_ref[...]
    for part in range(DEPTH_PARTS):
        half = DEPTH_ORDER[part] % 2
        out_ref[part] = field[:, half * LANES : (half + 1) * LANES]
    for load in loads[2:]:
        load.wait()


def depth_kernel(fields_ref, table_ref, out_ref):
    modes = table_first(table_ref[...], fields_ref[...])
    for slot in range(MODES):
        out_ref[pl.ds(slot, PAIR_SIZE, stride=MODES), :] = modes[
            slot * PAIR_SIZE : (slot + 1) * PAIR_SIZE
        ]


def strike_kernel(modes_ref, coarse_ref, fine_ref, back_ref, out_table, class_ref, out_ref):
    cosine, sine = class_ref[0], class_ref[1]
    depth_pos, strike_pos = lax.axis_index("depth"), lax.axis_index("strike")
    place = (
        depth_pos % 2 * WEIGHTS["h"]
        + strike_pos // 16 * WEIGHTS["x"]
        + (strike_pos // 2 + 8 - Z_FIRST) % 8 * WEIGHTS["z"]
        + strike_pos % 2 * WEIGHTS["c"]
    )
    base = depth_pos // 2 * PAIR_MODES + place
    depth_index = class_ref[3] + base.astype(F32)
    depth_wave = 2.0 * math.pi / DEPTH * jnp.minimum(depth_index, DEPTH - depth_index)
    depth_square = depth_wave * depth_wave
    strike_square = class_ref[2]
    wave_square = strike_square + depth_square
    kernel = (
        (-0.5 / (DEPTH * STRIKE))
        * (strike_square * ELASTIC + depth_square)
        / jnp.sqrt(jnp.where(wave_square > 0, wave_square, 1.0))
    )
    coarse = table_first(coarse_ref[...], modes_ref[...])
    real, imag = coarse[:SPEC_ROWS], coarse[SPEC_ROWS:]
    turned = jnp.concatenate([real * cosine + imag * sine, imag * cosine - real * sine], 1)
    spectrum = table_last(turned, fine_ref[...])
    spectrum = spectrum * jnp.concatenate([kernel, kernel], 1)
    back = table_last(spectrum, back_ref[...])
    real, imag = back[:, :LANES], back[:, LANES:]
    turned = jnp.concatenate([real * cosine - imag * sine, imag * cosine + real * sine], 0)
    out_ref[...] = table_first(out_table[...], turned)


def depth_back_kernel(modes_ref, table_ref, out_hbm, out_ref, sems):
    modes = jnp.concatenate(
        [modes_ref[pl.ds(slot, PAIR_SIZE, stride=MODES), :] for slot in range(MODES)], 0
    )
    stores = []
    for part in range(BACK_CHUNKS):
        rows = slice(part * DEPTH // BACK_CHUNKS, (part + 1) * DEPTH // BACK_CHUNKS)
        out_ref[rows] = table_turned(table_ref[:, rows], modes)
        stores.append(pltpu.make_async_copy(out_ref.at[rows], out_hbm.at[rows], sems.at[part]))
        stores[-1].start()
    for store in stores:
        store.wait()


def final_kernel(parts_ref, numerator_ref, denominator_ref, out_ref):
    for half in range(2):
        lanes = slice(half * LANES, (half + 1) * LANES)
        one, two, three, four = (
            parts_ref[part] for part in range(DEPTH_PARTS) if DEPTH_ORDER[part] % 2 == half
        )
        filtered = (one + two) + (three + four)
        out_ref[:, lanes] = (filtered + numerator_ref[:, lanes]) / denominator_ref[:, lanes]


def stencil_kernel(
    speed_hbm,
    memory_hbm,
    clamping_hbm,
    effect_a_hbm,
    effect_b_hbm,
    ambient_hbm,
    heat_hbm,
    fluid_hbm,
    memory_hbm_out,
    numerator_out,
    denominator_out,
    heat_out,
    fluid_out,
    speed_ref,
    memory_ref,
    clamping_ref,
    effect_a_ref,
    effect_b_ref,
    ambient_ref,
    memory_out,
    heat_in,
    fluid_in,
    heat_change,
    fluid_change,
    in_sem,
    out_sem,
    plane_sem,
):
    plane_loads = [
        pltpu.make_async_copy(source, target, plane_sem.at[at])
        for at, (source, target) in enumerate(
            (
                (speed_hbm, speed_ref),
                (memory_hbm, memory_ref),
                (clamping_hbm, clamping_ref),
                (effect_a_hbm, effect_a_ref),
                (effect_b_hbm, effect_b_ref),
                (ambient_hbm, ambient_ref),
            )
        )
    ]
    memory_store = pltpu.make_async_copy(memory_out, memory_hbm_out, plane_sem.at[6])
    for load in plane_loads:
        load.start()

    def pieces(source, target, sems, which):
        return [
            pltpu.make_async_copy(
                source.at[:, pl.ds(part * BLOCK, BLOCK), :],
                target.at[:, pl.ds(part * BLOCK, BLOCK), :],
                sems.at[which, part],
            )
            for part in range(ROWS // BLOCK)
        ]

    heat_loads = pieces(heat_hbm, heat_in, in_sem, 0)
    fluid_loads = pieces(fluid_hbm, fluid_in, in_sem, 1)
    heat_stores = pieces(heat_change, heat_out, out_sem, 0)
    fluid_stores = pieces(fluid_change, fluid_out, out_sem, 1)
    for part in range(ROWS // BLOCK):
        fluid_loads[part].start()
        heat_loads[part].start()
    for load in plane_loads:
        load.wait()
    for part in range(ROWS // BLOCK):
        fluid_loads[part].wait()
        heat_loads[part].wait()
        for row in range(part * BLOCK, (part + 1) * BLOCK, 8):
            rows = slice(row, row + 8)
            speed, memory = speed_ref[rows], memory_ref[rows]
            effect_a, effect_b = effect_a_ref[rows], effect_b_ref[rows]
            ratio = memory / effect_a
            argument = 0.5 * speed * jnp.exp(ratio)
            friction = effect_a * jnp.log(argument + jnp.sqrt(argument * argument + 1.0))
            root_term = jnp.sqrt(4.0 * jnp.exp(-2.0 * ratio) + speed * speed)
            effective = clamping_ref[rows] - fluid_in[0, rows]
            traction = effective * friction
            power = HEAT_GAIN * traction * speed
            memory_change = effect_b * (jnp.exp((REF_FRICTION - memory) / effect_b) - speed)
            memory_out[rows] = memory_change
            heat, fluid = heat_in[0, rows], fluid_in[0, rows]
            heat_above, fluid_above = heat_in[1, rows], fluid_in[1, rows]
            heat_below, fluid_below = heat_above, fluid_above
            for point in range(POINTS):
                bent = heat_below - 2.0 * heat
                pressed = fluid_below - 2.0 * fluid
                if point + 1 < POINTS:
                    bent = bent + heat_above
                    pressed = pressed + fluid_above
                warmed = HEAT_DIFFUSIVITY * bent + math.exp(-((point / HEAT_WIDTH) ** 2)) * power
                pressed = FLUID_DIFFUSIVITY * pressed + FLUID_TOGGLE * warmed
                heat_change[point, rows] = warmed
                fluid_change[point, rows] = pressed
                if point == 0:
                    extra = (
                        friction * pressed - effective * (speed / root_term) * memory_change
                    )
                    numerator_out[rows] = extra + RELAXATION * (
                        ambient_ref[rows] - DAMPING * speed - traction
                    )
                    denominator_out[rows] = effective * effect_a / root_term + DAMPING
                heat_below, fluid_below = heat, fluid
                heat, fluid = heat_above, fluid_above
                if point + 2 < POINTS:
                    heat_above, fluid_above = heat_in[point + 2, rows], fluid_in[point + 2, rows]
        heat_stores[part].start()
        fluid_stores[part].start()
    memory_store.start()
    memory_store.wait()
    for part in range(ROWS // BLOCK):
        heat_stores[part].wait()
        fluid_stores[part].wait()


def whole(count):
    return [pl.BlockSpec(memory_space=pltpu.VMEM)] * count


def anywhere(count):
    return [pl.BlockSpec(memory_space=pltpu.HBM)] * count


def in_hbm(*arrays):
    return [pltpu.with_memory_space_constraint(jnp.asarray(x), pltpu.HBM) for x in arrays]


def cost(flops, moved):
    return pl.CostEstimate(flops=flops, bytes_accessed=moved, transcendentals=0)


def shape(*dims):
    return jax.ShapeDtypeStruct(dims, F32)


BLOCK = 16


def grant(mebibytes):
    return pltpu.CompilerParams(vmem_limit_bytes=mebibytes * 1024 * 1024)


def shards(
    sliding_speed,
    offset_displacement,
    contact_memory,
    clamping_traction,
    instant_effect_a,
    healing_effect_b,
    ambient_traction,
    heat_level,
    fluid_load,
):
    depth_forward = depth_table().reshape(PAIRS, PAIR_MODES, DEPTH)
    coarse_forward, coarse_inverse = coarse_tables()
    fine_forward, fine_inverse = fine_tables()
    small = ROWS * COLS * 4
    groups = [
        [(2 * pair + half) * STRIKE_PARTS + part for part, half in PIECES] for pair in range(PAIRS)
    ]

    def over_depth(pieces):
        return lax.all_to_all(
            pieces, "depth", split_axis=0, concat_axis=0, axis_index_groups=[DEPTH_ORDER]
        )

    def over_pair(pieces):
        pieces = pieces.reshape(PAIR_SIZE, 1, MODES * LANES)
        moved = lax.all_to_all(
            pieces, ("depth", "strike"), split_axis=0, concat_axis=0, axis_index_groups=groups
        )
        return moved.reshape(PAIR_ROWS, LANES)

    sent, depth_part = pl.pallas_call(
        field_kernel,
        out_shape=(
            shape(DEPTH_PARTS, ROWS, LANES),
            pltpu.VMEM((2 * PAIR_MODES, DEPTH), BF16),
        ),
        in_specs=anywhere(3),
        out_specs=whole(2),
        scratch_shapes=[pltpu.VMEM((ROWS, COLS), F32)] * 2
        + [pltpu.SemaphoreType.DMA((2 + TABLE_CHUNKS,))],
        compiler_params=grant(4),
        cost_estimate=cost(2 * ROWS * COLS, 12 * small),
    )(*in_hbm(sliding_speed, offset_displacement, halves(depth_forward)))
    columns = over_depth(sent)

    modes = pl.pallas_call(
        depth_kernel,
        out_shape=shape(PAIR_ROWS, LANES),
        in_specs=whole(2),
        out_specs=pl.BlockSpec(memory_space=pltpu.VMEM),
        compiler_params=grant(10),
        cost_estimate=cost(6 * PAIR_MODES * DEPTH * LANES, 12 * small),
    )(columns.reshape(DEPTH, LANES), depth_part)

    filtered = pl.pallas_call(
        strike_kernel,
        out_shape=shape(PAIR_ROWS, LANES),
        in_specs=whole(6),
        out_specs=pl.BlockSpec(memory_space=pltpu.VMEM),
        compiler_params=grant(6),
        cost_estimate=cost(6 * 4 * 256 * 256 * LANES, 15 * small),
    )(
        over_pair(modes),
        halves(coarse_forward),
        halves(fine_forward),
        halves(fine_inverse),
        halves(coarse_inverse),
        class_tables(),
    )

    sent = pl.pallas_call(
        depth_back_kernel,
        out_shape=shape(DEPTH, LANES),
        in_specs=whole(2),
        out_specs=pl.BlockSpec(memory_space=pltpu.HBM),
        scratch_shapes=[pltpu.VMEM((DEPTH, LANES), F32), pltpu.SemaphoreType.DMA((BACK_CHUNKS,))],
        compiler_params=grant(10),
        cost_estimate=cost(6 * PAIR_MODES * DEPTH * LANES, 12 * small),
    )(over_pair(filtered), depth_part)
    parts = over_depth(sent.reshape(DEPTH_PARTS, ROWS, LANES))

    memory_change, numerator, denominator, heat_level_change, fluid_load_change = pl.pallas_call(
        stencil_kernel,
        out_shape=(
            shape(ROWS, COLS),
            pltpu.VMEM((ROWS, COLS), F32),
            pltpu.VMEM((ROWS, COLS), F32),
            shape(POINTS, ROWS, COLS),
            shape(POINTS, ROWS, COLS),
        ),
        in_specs=anywhere(8),
        out_specs=anywhere(1) + whole(2) + anywhere(2),
        scratch_shapes=[pltpu.VMEM((ROWS, COLS), F32)] * 7
        + [pltpu.VMEM((POINTS, ROWS, COLS), F32)] * 4
        + [pltpu.SemaphoreType.DMA((2, ROWS // BLOCK))] * 2
        + [pltpu.SemaphoreType.DMA((7,))],
        compiler_params=grant(20),
        cost_estimate=cost(18 * POINTS * ROWS * COLS, 137 * small),
    )(
        *in_hbm(
            sliding_speed,
            contact_memory,
            clamping_traction,
            instant_effect_a,
            healing_effect_b,
            ambient_traction,
            heat_level,
            fluid_load,
        )
    )

    sliding_acceleration = pl.pallas_call(
        final_kernel,
        out_shape=shape(ROWS, COLS),
        in_specs=whole(3),
        out_specs=pl.BlockSpec(memory_space=pltpu.VMEM),
        compiler_params=grant(4),
        cost_estimate=cost(5 * ROWS * COLS, 7 * small),
    )(parts, numerator, denominator)
    return (sliding_acceleration, memory_change, heat_level_change, fluid_load_change)


def solution(mesh):
    plane = P("depth", "strike")
    block = P(None, "depth", "strike")
    return jax.shard_map(
        shards,
        mesh=mesh,
        in_specs=(plane,) * 7 + (block,) * 2,
        out_specs=(plane, plane, block, block),
        check_vma=False,
    )
```
